128 devices in a mesh: slab: 32 (over y, z, x_lo), run: 4 (over x_hi, core).
Axes of the slice: x: 4 (x_hi: 2, x_lo: 2; x = x_hi * 2 + x_lo), y: 4, z: 4, core: 2. Of those that a mesh axis runs over, the one named last changes fastest.
Arguments:
- material: int32 [128, 256, 256], P('slab'), may hold values from 0 to 15
- eps_table: float32 [16], replicated, may hold values from 1 to 12
- surface_mask: int32 [128], P('slab'), may hold values 0 or 1
- excite_map: int32 [4], P('run'), may hold values from 0 to 3
- mode_profiles: float32 [4, 256, 256], P(None, 'slab'), may hold values from -4 to 4
- port_eps: float32 [256, 256], P('slab'), may hold values from 1 to 4
- cotangent: float32 [4, 128, 256, 256], P('run', 'slab'), may hold values from -6 to 6
Outputs:
- gradient: float32 [128, 256, 256], P('slab')
- field_out: float32 [4, 128, 256, 256], P('run', 'slab')
The draws below stay inside these ranges and needn't reach their ends.
Inputs may be any that keep to these rules, and one draw needn't show every extreme that they name: material indices into the permittivity table. `surface_mask`: 0 or 1 for each x layer. `excite_map`: an index of a mode profile.
All inputs are finite; a program needn't handle non-finite values. No bound on the sum of `surface_mask` on one device may be relied on, other than what follows from the above.
Results may differ from the reference program's by a relative error of at most 0.0001.
Values sent between devices are 32-bit elements; how exact they have to be, the bound alone decides.
A program may use at most 128 MiB of HBM per device.

```python
import math
import jax
import jax.numpy as jnp
from jax import lax

NY = 256
NZ = 256
STEPS = 6
NMAT = 16
NEXC = 4
NX = 128
RUNS = 4


def place_ends(entries, own_key, smallest, largest):
    longest = entries.shape.index(max(entries.shape))
    spots = []
    for shift in (0, 1):
        where = [jax.random.randint(jax.random.fold_in(own_key, axis), (), 0, length) for axis, length in enumerate(entries.shape)]
        where[longest] = (where[longest] + shift) % entries.shape[longest]
        spots.append(tuple(where))
    return entries.at[spots[0]].set(smallest).at[spots[1]].set(largest)


def block_scale(rng, extent, split, smallest, largest):
    factor_of = 1.0
    for dim, parts in split:
        heights = jax.random.uniform(jax.random.fold_in(jax.random.fold_in(rng, 6), dim), (parts,), jnp.float32, smallest / len(split), largest / len(split))
        factor_of = factor_of * jnp.repeat(jnp.exp(heights), extent[dim] // parts).reshape((-1,) + (1,) * (len(extent) - 1 - dim))
    return factor_of


def centred(rng, extent, width, reach, pieces=(), kind=jnp.bfloat16):
    values = jax.random.normal(rng, extent, jnp.float32) * width
    if len(pieces) > 0:
        values = block_scale(rng, extent, pieces, -0.22, 0.18) * values
    return jnp.clip(values, min=-reach, max=reach).astype(kind)


def setup_inputs(seed: int = 0) -> dict:
    keys = jax.random.split(jax.random.key(seed), 8)
    material = place_ends(jax.random.randint(keys[0], (NX, NY, NZ), 0, NMAT), jax.random.fold_in(keys[0], 1), 0, NMAT - 1).astype(jnp.int32)
    eps_table = jnp.clip(jnp.exp(jax.random.uniform(keys[1], (NMAT,), jnp.float32, math.log(1.0), math.log(12.0))), 1.0, 12.0)
    surface_mask = place_ends((jax.random.randint(keys[2], (NX,), 0, 8) < 1).astype(jnp.int32), jax.random.fold_in(keys[2], 1), 0, 1)
    excite_map = place_ends(jax.random.randint(keys[3], (RUNS,), 0, NEXC), jax.random.fold_in(keys[3], 1), 0, NEXC - 1).astype(jnp.int32)
    mode_profiles = centred(keys[4], (NEXC, NY, NZ), 1.0, 4.0, ((1, 32),), jnp.float32)
    port_eps = jnp.clip(jnp.exp(math.log(4.0) - 1.3862944 * jax.random.uniform(keys[5], (NY, NZ), jnp.float32) ** block_scale(keys[5], (NY, NZ), ((0, 32),), -0.2, 0.2)), 1.0, 4.0)
    cotangent = centred(keys[6], (RUNS, NX, NY, NZ), 1.0, 6.0, ((0, 4), (1, 32)), jnp.float32)
    return {"material": material, "eps_table": eps_table, "surface_mask": surface_mask, "excite_map": excite_map, "mode_profiles": mode_profiles, "port_eps": port_eps, "cotangent": cotangent}


time_step = 0.5


def rim_zero(field, along):
    return jnp.zeros_like(lax.slice_in_dim(field, 0, 1, axis=along))


def ahead(field, along, border):
    length = field.shape[along]
    return jnp.concatenate([lax.slice_in_dim(field, 1, length, axis=along), border], along) - field


def behind(field, along, border):
    length = field.shape[along]
    return field - jnp.concatenate([border, lax.slice_in_dim(field, 0, length - 1, axis=along)], along)


def update_magnetic(electric, magnetic, upper_y, upper_z):
    electric_x, electric_y, electric_z = electric
    magnetic_x, magnetic_y, magnetic_z = magnetic
    magnetic_x = magnetic_x - time_step * (ahead(electric_z, 2, rim_zero(electric_z, 2)) - ahead(electric_y, 3, rim_zero(electric_y, 3)))
    magnetic_y = magnetic_y - time_step * (ahead(electric_x, 3, rim_zero(electric_x, 3)) - ahead(electric_z, 1, upper_z))
    magnetic_z = magnetic_z - time_step * (ahead(electric_y, 1, upper_y) - ahead(electric_x, 2, rim_zero(electric_x, 2)))
    return magnetic_x, magnetic_y, magnetic_z


def update_electric(electric, magnetic, lower_y, lower_z, coefficient, source_y, source_z):
    electric_x, electric_y, electric_z = electric
    magnetic_x, magnetic_y, magnetic_z = magnetic
    electric_x = electric_x + coefficient * (behind(magnetic_z, 2, rim_zero(magnetic_z, 2)) - behind(magnetic_y, 3, rim_zero(magnetic_y, 3)))
    electric_y = electric_y + coefficient * (behind(magnetic_x, 3, rim_zero(magnetic_x, 3)) - behind(magnetic_z, 1, lower_z)) + source_y
    electric_z = electric_z + coefficient * (behind(magnetic_y, 1, lower_y) - behind(magnetic_x, 2, rim_zero(magnetic_x, 2))) + source_z
    return electric_x, electric_y, electric_z


def modal_advance(modal_now, modal_old, padded, port_coefficient, profile, forcing):
    middle = padded[1:-1]
    zpadded = jnp.pad(middle, ((0, 0), (1, 1)))
    laplacian = padded[2:] + padded[:-2] + zpadded[:, 2:] + zpadded[:, :-2] - 4.0 * middle
    return 2.0 * modal_now - modal_old + port_coefficient * laplacian + forcing * profile


def forcing_at(counter):
    moment = (counter + 1).astype(jnp.float32)
    return 2.0 * jnp.sin(0.3 * moment) * (1.0 - jnp.exp(-0.5 * moment))


def permittivity_of(material, eps_table):
    levels = jnp.arange(eps_table.shape[0], dtype=jnp.int32)
    picked = (material[None] == levels[:, None, None, None]).astype(jnp.float32)
    return jnp.sum(picked * eps_table[:, None, None, None], axis=0)


def reference(material, eps_table, surface_mask, excite_map, mode_profiles, port_eps, cotangent):
    coefficient = time_step / permittivity_of(material, eps_table)
    mask_column = surface_mask.astype(jnp.float32)[:, None, None]
    port_coefficient = 0.25 / port_eps
    injection = 0.25 * coefficient * mask_column
    selector = jnp.array([1.0, 0.0], jnp.float32)[:, None, None, None]
    total = jnp.zeros(coefficient.shape, jnp.float32)
    fields = []
    for runner in range(RUNS):
        choose = (jnp.arange(NEXC, dtype=jnp.int32) == excite_map[runner]).astype(jnp.float32)
        profile = jnp.sum(mode_profiles * choose[:, None, None], axis=0)
        zeros = jnp.zeros((2,) + coefficient.shape, jnp.float32)
        electric = (zeros.at[0].set(cotangent[runner]), zeros, zeros.at[1].set(cotangent[runner]))
        magnetic = (zeros, zeros, zeros)
        modal_zero = jnp.zeros(profile.shape, jnp.float32)

        def advance(counter, carried):
            electric, magnetic, modal_now, modal_old, gradient_sum = carried
            forcing = forcing_at(counter)
            padded = jnp.pad(modal_now, ((1, 1), (0, 0)))
            modal_next = modal_advance(modal_now, modal_old, padded, port_coefficient, profile, forcing)
            incident_e = modal_next
            incident_h = modal_next - modal_now
            upper = rim_zero(electric[1], 1)
            magnetic = update_magnetic(electric, magnetic, upper, upper)
            lower = rim_zero(magnetic[1], 1)
            electric = update_electric(electric, magnetic, lower, lower, coefficient, selector * (injection * incident_h), selector * (injection * incident_e))
            gradient_sum = gradient_sum + (electric[0][0] * electric[0][1] + electric[1][0] * electric[1][1] + electric[2][0] * electric[2][1])
            return electric, magnetic, modal_next, modal_now, gradient_sum

        carried = lax.fori_loop(0, STEPS, advance, (electric, magnetic, modal_zero, modal_zero, jnp.zeros(coefficient.shape, jnp.float32)))
        total = total + carried[4]
        fields.append(carried[0][1][0])
    return total, jnp.stack(fields)
```

```python
import functools
import math

import jax
import jax.numpy as jnp
from jax import lax
from jax.experimental import pallas as pl
from jax.experimental.pallas import tpu as pltpu
from jax.sharding import PartitionSpec as P

STEPS = 6
F32 = jnp.float32
DEPTH = 4
LAYERS = 2 * DEPTH + 2 * STEPS
PAD = 8
FIRST = STEPS
LOOK = 4


def forcing_of(n):
    t = float(n + 1)
    return 2.0 * math.sin(0.3 * t) * (1.0 - math.exp(-0.5 * t))


def cuts(total, sizes):
    spans, at = [], 0
    for size in sizes:
        if at < total:
            spans.append((at, min(total, at + size)))
            at += size
    if at < total:
        spans.append((at, total))
    return spans


def kernel(
    slabs, grid_y, grid_z,
    eps_s, mask_s, excite_s, profiles_v, port_v, material_h, cot_h,
    grad_h, out_h,
    C, K, SK, MT, EX, EY, EZ, GX, GY, GZ, GR, W, gath, near, part, far, side, fin,
    load_sem, ag_send, ag_recv, xc_send, xc_recv, xk_send, xk_recv, z_send, z_recv,
    near_send, near_recv, far_send, far_recv, fin_copy, fin_send, fin_recv, fo_copy, fo_send, fo_recv,
):
    half = 4 * slabs
    tiles = slabs // 2 + 1
    rows_all = 8 * tiles
    pairs = slabs // 2
    in_chunks = cuts(tiles, (3, 3, 4, 4, 3))
    out_chunks = cuts(tiles - 1, (6, 5, 3, 2))
    s = lax.axis_index("slab")
    r = lax.axis_index("run")
    p = lax.rem(s, 2)
    m = s // 2
    core = lax.rem(r, 2)
    other_core = r + 1 - 2 * core
    other_run = lax.rem(r + 2, 4)
    mate = s + 1 - 2 * p
    py, pz = m // grid_z, lax.rem(m, grid_z)
    not_first, not_last = m > 0, m < pairs - 1
    window = p * (slabs // 2 - 1)
    base, mate_base = 8 * window, 8 * ((1 - p) * (slabs // 2 - 1))
    own, mates = FIRST + DEPTH * p, FIRST + DEPTH * (1 - p)

    def to(slab, run):
        return {"slab": slab, "run": run}

    def remote(src, dst, send, recv, slab, run):
        return pltpu.make_async_remote_copy(
            src_ref=src, dst_ref=dst, send_sem=send, recv_sem=recv,
            device_id=to(slab, run), device_id_type=pl.DeviceIdType.MESH,
        )

    def lanes(h):
        return pl.ds(128 * h, 128)

    def ds8(start, size):
        return pl.ds(pl.multiple_of(start, 8), size)

    loads = []
    for h in range(2):
        loads.append(pltpu.make_async_copy(material_h.at[:, :, lanes(h)], MT.at[:, h], load_sem.at[h]))
        loads.append(
            pltpu.make_async_copy(
                cot_h.at[0, :, ds8(base, rows_all), lanes(h)],
                C.at[pl.ds(own, DEPTH), h, pl.ds(PAD, rows_all), :],
                load_sem.at[2 + h],
            )
        )
    for copy in loads:
        copy.start()

    z_mates = [(py * grid_z + lax.rem(pz + d, grid_z)) * 2 + p for d in range(1, grid_z)]
    y_mates = [(lax.rem(py + d, grid_y) * grid_z + pz) * 2 + p for d in range(1, grid_y)]
    barrier = pltpu.get_barrier_semaphore()

    def hello(slab, run):
        pl.semaphore_signal(barrier, inc=1, device_id=to(slab, run), device_id_type=pl.DeviceIdType.MESH)

    hello(mate, r)
    hello(mate, other_run)
    hello(s, other_core)
    hello(s, other_run)
    for peer in z_mates + y_mates:
        hello(peer, r)

    @pl.when(not_first)
    def _():
        hello(s - 2, r)

    @pl.when(not_last)
    def _():
        hello(s + 2, r)

    picked = jnp.zeros((8, 256), F32)
    for j in range(4):
        picked = jnp.where(excite_s[0] == j, profiles_v[j], picked)
    port = 0.25 / port_v[...]
    for h in range(2):
        gath[s, h] = picked[:, 128 * h : 128 * h + 128]
        gath[s, 2 + h] = port[:, 128 * h : 128 * h + 128]

    zero_row = jnp.zeros((8, 128), F32)
    bottom = jnp.zeros((2, 2, 8, 128), F32)

    def clear(i, carry):
        C[i, :, pl.ds(PAD + rows_all, 8), :] = jnp.zeros((2, 8, 128), F32)
        return carry

    lax.fori_loop(0, LAYERS, clear, 0)

    def clear_fields(i, carry):
        EX[i, :, :, pl.ds(PAD + rows_all, 8), :] = bottom
        EZ[i, :, :, pl.ds(PAD + rows_all, 8), :] = bottom
        GX[i, :, :, pl.ds(0, 8), :] = bottom
        GZ[i, :, :, pl.ds(0, 8), :] = bottom
        return carry

    lax.fori_loop(0, LAYERS - 2, clear_fields, 0)
    GX[LAYERS - 2, :, :, pl.ds(0, 8), :] = bottom
    GZ[LAYERS - 2, :, :, pl.ds(0, 8), :] = bottom
    for n in range(STEPS):
        for edge in (0, PAD + rows_all):
            W[n, :, pl.ds(edge, 8), :] = jnp.zeros((2, 8, 128), F32)

    def clear_end(c_first, k_first):
        def one(t, carry):
            rows = ds8(8 * t, 8)
            C[pl.ds(c_first, STEPS), :, rows, :] = jnp.zeros((STEPS, 2, 8, 128), F32)
            K[pl.ds(k_first, STEPS - 1), :, rows, :] = jnp.zeros((STEPS - 1, 2, 8, 128), F32)
            return carry

        lax.fori_loop(0, tiles + 1, one, 0)

    @pl.when(m == 0)
    def _():
        clear_end(0, 0)

    @pl.when(m == pairs - 1)
    def _():
        clear_end(FIRST + 2 * DEPTH, FIRST + 2 * DEPTH - 1)

    def k_rows(c):
        start, stop = in_chunks[c]
        first = 0 if c == 0 else PAD + 8 * start
        return pl.ds(first, PAD + 8 * stop - first)

    def c_rows(c):
        start, stop = in_chunks[c]
        return pl.ds(PAD + 8 * start, 8 * (stop - start))

    for j in range(DEPTH):
        tile = jnp.full((8, 128), mask_s[j].astype(F32), F32)
        for h in range(2):
            SK[j, h, pl.ds(0, 8), :] = tile
            K[own - 1 + j, h, pl.ds(0, 8), :] = tile

    pl.semaphore_wait(
        barrier, 4 + (grid_z - 1) + (grid_y - 1) + not_first.astype(jnp.int32) + not_last.astype(jnp.int32)
    )

    ag_pair = remote(gath.at[s], gath.at[s], ag_send.at[0], ag_recv.at[0], mate, r)
    ag_pair.start()
    xc = []
    for c in range(len(in_chunks)):
        start, stop = in_chunks[c]
        for h in range(2):
            copy = remote(
                cot_h.at[0, :, ds8(mate_base + 8 * start, 8 * (stop - start)), lanes(h)],
                C.at[pl.ds(own, DEPTH), h, c_rows(c), :],
                xc_send.at[c, h], xc_recv.at[c, h], mate, r,
            )
            copy.start()
            xc.append(copy)

    table = [0.25 / jnp.full((1, 1, 8, 128), eps_s[j], F32) for j in range(16)]

    def coefficient_of(index):
        level = table
        for bit in range(4):
            odd = ((index >> bit) & 1) != 0
            level = [jnp.where(odd, level[2 * j + 1], level[2 * j]) for j in range(len(level) // 2)]
        return level[0]

    loads[0].wait()
    loads[2].wait()
    xk = []
    for c in range(len(in_chunks)):
        start, stop = in_chunks[c]

        def mates_rows(t, carry):
            SK[:, :, ds8(PAD + 8 * t, 8), :] = coefficient_of(MT[:, :, ds8(mate_base + 8 * t, 8), :])
            return carry

        lax.fori_loop(start, stop, mates_rows, 0)
        copy = remote(
            SK.at[:, :, k_rows(c), :], K.at[pl.ds(own - 1, DEPTH), :, k_rows(c), :],
            xk_send.at[c], xk_recv.at[c], mate, other_run,
        )
        copy.start()
        xk.append(copy)

    def own_rows(t, carry):
        K[pl.ds(own - 1, DEPTH), :, ds8(PAD + 8 * t, 8), :] = coefficient_of(MT[:, :, ds8(base + 8 * t, 8), :])
        return carry

    lax.fori_loop(0, tiles, own_rows, 0)

    remote(gath.at[mate], gath.at[mate], ag_send.at[0], ag_recv.at[0], mate, r).wait_recv()
    ag_z = []
    for d in range(1, grid_z):
        copy = remote(
            gath.at[pl.ds(2 * m, 2)], gath.at[pl.ds(2 * m, 2)], ag_send.at[d], ag_recv.at[d], z_mates[d - 1], r
        )
        copy.start()
        ag_z.append(copy)

    loads[1].wait()
    loads[3].wait()

    def z_copy(c, kind, up):
        if kind == 0:
            ref, rows, size = C, c_rows(c), STEPS
            src, dst = (FIRST + 2, 0) if up else (FIRST, FIRST + 2 * DEPTH)
        else:
            ref, rows, size = K, k_rows(c), STEPS - 1
            src, dst = (FIRST + 2, 0) if up else (FIRST - 1, FIRST + 2 * DEPTH - 1)
        way = 0 if up else 1
        return remote(
            ref.at[pl.ds(src, size), :, rows, :], ref.at[pl.ds(dst, size), :, rows, :],
            z_send.at[way, kind, c], z_recv.at[way, kind, c], s + 2 if up else s - 2, r,
        )

    def pass_on(c):
        start, stop = in_chunks[c]
        for h in range(2):
            remote(
                cot_h.at[0, :, ds8(mate_base + 8 * start, 8 * (stop - start)), lanes(h)],
                C.at[pl.ds(mates, DEPTH), h, c_rows(c), :],
                xc_send.at[c, h], xc_recv.at[c, h], mate, r,
            ).wait_recv()
        remote(
            SK.at[:, :, k_rows(c), :], K.at[pl.ds(mates - 1, DEPTH), :, k_rows(c), :],
            xk_send.at[c], xk_recv.at[c], mate, other_run,
        ).wait_recv()

        @pl.when(not_last)
        def _():
            for kind in range(2):
                z_copy(c, kind, True).start()

        @pl.when(not_first)
        def _():
            for kind in range(2):
                z_copy(c, kind, False).start()

    def halo_wait(c):
        @pl.when(not_first)
        def _():
            for kind in range(2):
                z_copy(c, kind, True).wait_recv()

        @pl.when(not_last)
        def _():
            for kind in range(2):
                z_copy(c, kind, False).wait_recv()

    pass_on(0)

    for d in range(1, grid_z):
        source = (py * grid_z + lax.rem(pz - d + grid_z, grid_z)) * 2
        remote(
            gath.at[pl.ds(source, 2)], gath.at[pl.ds(source, 2)], ag_send.at[d], ag_recv.at[d], z_mates[d - 1], r
        ).wait_recv()

    group = 2 * grid_z

    def whole(y):
        return jnp.where(p == 0, y < grid_y // 2, y >= grid_y // 2)

    def single(y):
        return y == grid_y // 2 - p

    single_slot = slabs // 2 - p

    def y_copy(d, y, full):
        slots = pl.ds(group * y, group) if full else pl.ds(single_slot, 1)
        return remote(
            gath.at[slots], gath.at[slots], ag_send.at[grid_z + d - 1], ag_recv.at[grid_z + d - 1], y_mates[d - 1], r
        )

    def y_each(y, action):
        @pl.when(whole(y))
        def _():
            action(True)

        @pl.when(single(y))
        def _():
            action(False)

    for d in range(1, grid_y):
        y_each(py, lambda full: y_copy(d, py, full).start())
    for c in range(1, len(in_chunks)):
        if in_chunks[c][0] - 1 - LOOK < 0:
            pass_on(c)
    for d in range(1, grid_y):
        source = lax.rem(py - d + grid_y, grid_y)
        y_each(source, lambda full: y_copy(d, source, full).wait_recv())

    lane = lax.broadcasted_iota(jnp.int32, (1, 1, 8, 128), 3)
    is_last, is_first = lane == 127, lane == 0

    def up_z(v):
        turned = pltpu.roll(v, 127, v.ndim - 1)
        follow = jnp.concatenate([turned[1:2], jnp.zeros_like(turned[1:2])], 0)
        return jnp.where(is_last if v.ndim == 4 else is_last[0], follow, turned)

    def down_z(v):
        turned = pltpu.roll(v, 1, v.ndim - 1)
        before = jnp.concatenate([jnp.zeros_like(turned[0:1]), turned[0:1]], 0)
        return jnp.where(is_first if v.ndim == 4 else is_first[0], before, turned)

    for n in range(STEPS):

        def port_rows(t, carry):
            rows = ds8(PAD + 8 * t, 8)
            slot = window + t
            drive = (0.5 * forcing_of(n)) * gath[slot, pl.ds(0, 2)]
            if n == 0:
                W[0, :, rows, :] = drive
                return carry
            now = W[n - 1, :, rows, :]
            after = W[n - 1, :, pl.ds(PAD + 8 * t + 1, 8), :]
            before = W[n - 1, :, pl.ds(PAD + 8 * t - 1, 8), :]
            laplacian = after + before + up_z(now) + down_z(now) - 4.0 * now
            value = 2.0 * now + gath[slot, pl.ds(2, 2)] * laplacian + drive
            if n > 1:
                value = value - W[n - 2, :, rows, :]
            W[n, :, rows, :] = value
            return carry

        lax.fori_loop(0, tiles, port_rows, 0)

    inside = not_first.astype(F32)

    def source_of(n, rows):
        ie = W[n - 1, :, rows, :]
        ih = ie if n == 1 else ie - W[n - 2, :, rows, :]
        return ie, ih

    def add_driven(v, extra):
        return jnp.concatenate([v[:, 0:1] + extra[:, None], v[:, 1:2]], 1)

    def product(a):
        return a[:, 0] * a[:, 1]

    def first_step(t):
        rows = ds8(PAD + 8 * t, 8)
        ahead_rows, behind_rows = pl.ds(PAD + 8 * t + 1, 8), pl.ds(PAD + 8 * t - 1, 8)
        ie, ih = source_of(1, rows)
        zero = jnp.zeros((2, 8, 128), F32)
        both = lambda d, e: jnp.stack([d, e], 1)
        follow = C[0, :, rows, :]
        gx_l = gy_l = gyd_l = None
        for i in range(LAYERS - 1):
            c = follow
            follow = C[i + 1, :, rows, :]
            gx = c - C[i, :, ahead_rows, :]
            gy = follow - c
            gyd = c - up_z(c)
            GX[i, :, :, rows, :] = both(zero, gx)
            GY[i, :, :, rows, :] = both(gyd, gy)
            GZ[i, :, :, rows, :] = both(-gx, zero)
            if i >= 1:
                if i == FIRST:
                    gx_l, gy_l, gyd_l = gx_l * inside, gy_l * inside, gyd_l * inside
                k = K[i - 1, :, rows, :]
                mask = K[i - 1, 0:1, pl.ds(0, 8), :]
                gx_y = gx - GX[i, :, 1, behind_rows, :]
                ex_d = c - k * (gx_y + (gyd - down_z(gyd)))
                ey_d = k * ((gx - gx_l) + mask * ih)
                ez_d = k * ((gyd - gyd_l) + mask * ie)
                ex_s = k * (down_z(gy) - gy)
                ey_s = k * (gx - down_z(gx))
                ez_s = c + k * ((gy - gy_l) - gx_y)
                EX[i - 1, :, :, rows, :] = both(ex_d, ex_s)
                EY[i - 1, :, :, rows, :] = both(ey_d, ey_s)
                EZ[i - 1, :, :, rows, :] = both(ez_d, ez_s)
                if FIRST <= i < FIRST + 2 * DEPTH:
                    GR[i - FIRST, :, rows, :] = ex_d * ex_s + ey_d * ey_s + ez_d * ez_s
            gx_l, gy_l, gyd_l = gx, gy, gyd

    def later_step(n, t):
        rows = ds8(PAD + 8 * t, 8)
        ahead_rows, behind_rows = pl.ds(PAD + 8 * t + 1, 8), pl.ds(PAD + 8 * t - 1, 8)
        ie, ih = source_of(n, rows)
        ey_n, ez_n = EY[n - 2, :, :, rows, :], EZ[n - 2, :, :, rows, :]
        gy_l = gz_l = None
        for i in range(n - 1, LAYERS - n):
            ex, ey, ez = EX[i - 1, :, :, rows, :], ey_n, ez_n
            ey_n, ez_n = EY[i, :, :, rows, :], EZ[i, :, :, rows, :]
            gx = GX[i, :, :, rows, :] + ((ez - EZ[i - 1, :, :, ahead_rows, :]) + (up_z(ey) - ey))
            gy = GY[i, :, :, rows, :] + ((ex - up_z(ex)) + (ez_n - ez))
            gz = GZ[i, :, :, rows, :] + ((ey - ey_n) + (EX[i - 1, :, :, ahead_rows, :] - ex))
            GX[i, :, :, rows, :] = gx
            GY[i, :, :, rows, :] = gy
            GZ[i, :, :, rows, :] = gz
            if i >= n:
                if i == FIRST:
                    gy_l, gz_l = gy_l * inside, gz_l * inside
                k = K[i - 1, :, rows, :][:, None]
                mask = K[i - 1, 0:1, pl.ds(0, 8), :]
                ex = ex + k * ((gz - GZ[i, :, :, behind_rows, :]) - (gy - down_z(gy)))
                ey = ey + k * add_driven((gx - down_z(gx)) - (gz - gz_l), mask * ih)
                ez = ez + k * add_driven((gy - gy_l) - (gx - GX[i, :, :, behind_rows, :]), mask * ie)
                EX[i - 1, :, :, rows, :] = ex
                EY[i - 1, :, :, rows, :] = ey
                EZ[i - 1, :, :, rows, :] = ez
                if FIRST <= i < FIRST + 2 * DEPTH:
                    GR[i - FIRST, :, rows, :] = GR[i - FIRST, :, rows, :] + (product(ex) + product(ey) + product(ez))
            gy_l, gz_l = gy, gz

    def near_copy(j):
        first, stop = out_chunks[j]
        return remote(
            GR.at[:, 1 - core, ds8(PAD + 8 * (p + first), 8 * (stop - first)), :],
            near.at[:, pl.ds(8 * first, 8 * (stop - first)), :],
            near_send.at[j], near_recv.at[j], s, other_core,
        )

    def far_copies(j):
        first, stop = out_chunks[j]
        rows = pl.ds(8 * first, 8 * (stop - first))
        mine, theirs = pl.ds(DEPTH * p, DEPTH), pl.ds(DEPTH * (1 - p), DEPTH)
        return [
            remote(part.at[mine, rows, :], far.at[:, rows, :], far_send.at[0, j], far_recv.at[0, j], s, other_run),
            remote(part.at[theirs, rows, :], side.at[0, :, rows, :], far_send.at[1, j], far_recv.at[1, j], mate, r),
            remote(
                part.at[theirs, rows, :], side.at[1, :, rows, :], far_send.at[2, j], far_recv.at[2, j], mate, other_run
            ),
        ]

    def fin_copies(j):
        first, stop = out_chunks[j]
        copies = []
        for k in range(2):
            rows = ds8(half * k + 8 * first, 8 * (stop - first))
            src = fin.at[:, rows, :]
            dst = grad_h.at[:, rows, pl.ds(pl.multiple_of(128 * core, 128), 128)]
            copies.append(
                (
                    pltpu.make_async_copy(src, dst, fin_copy.at[k, j]),
                    remote(src, dst, fin_send.at[k, j], fin_recv.at[k, j], s, other_core),
                    remote(
                        src, grad_h.at[:, rows, pl.ds(pl.multiple_of(128 * (1 - core), 128), 128)],
                        fin_send.at[k, j], fin_recv.at[k, j], s, other_core,
                    ),
                )
            )
        return copies

    def field_copies(j):
        first, stop = out_chunks[j]
        size = 8 * (stop - first)
        copies = []
        for h in range(2):
            src_rows = ds8(PAD + 8 * (p + first), size)
            dst = out_h.at[0, :, ds8(half * p + 8 * first, size), lanes(h)]
            back = out_h.at[0, :, ds8(half * (1 - p) + 8 * first, size), lanes(h)]
            src = EY.at[pl.ds(mates - 1, DEPTH), h, 0, src_rows, :]
            copies.append(
                (
                    pltpu.make_async_copy(EY.at[pl.ds(own - 1, DEPTH), h, 0, src_rows, :], dst, fo_copy.at[h, j]),
                    remote(src, dst, fo_send.at[h, j], fo_recv.at[h, j], mate, r),
                    remote(src, back, fo_send.at[h, j], fo_recv.at[h, j], mate, r),
                )
            )
        return copies

    def rows_done(j):
        near_copy(j).start()
        for here, there, _ in field_copies(j):
            there.start()
            here.start()

    def sum_cores(j):
        first, stop = out_chunks[j]
        near_copy(j).wait_recv()

        def one(t, carry):
            rows = ds8(8 * t, 8)
            part[:, rows, :] = GR[:, core, ds8(PAD + 8 * (p + t), 8), :] + near[:, rows, :]
            return carry

        lax.fori_loop(first, stop, one, 0)
        for copy in far_copies(j):
            copy.start()

    def sum_chips(j):
        first, stop = out_chunks[j]
        for copy in far_copies(j):
            copy.wait_recv()

        def one(t, carry):
            rows = ds8(8 * t, 8)
            fin[:, ds8(half * p + 8 * t, 8), :] = part[pl.ds(DEPTH * p, DEPTH), rows, :] + far[:, rows, :]
            fin[:, ds8(half * (1 - p) + 8 * t, 8), :] = side[0, :, rows, :] + side[1, :, rows, :]
            return carry

        lax.fori_loop(first, stop, one, 0)
        for here, there, _ in fin_copies(j):
            there.start()
            here.start()

    sweeps = tiles + STEPS - 1
    before, after, late = {}, {}, []
    for c in range(1, len(in_chunks)):
        at = in_chunks[c][0] - 1
        if at - LOOK >= 0:
            before.setdefault(at - LOOK, []).append(functools.partial(pass_on, c))
        before.setdefault(at, []).append(functools.partial(halo_wait, c))
    for j in range(len(out_chunks)):
        at = out_chunks[j][1] + STEPS - 1
        for event, delay in ((rows_done, 0), (sum_cores, 2), (sum_chips, 5)):
            if at + delay < sweeps:
                after.setdefault(at + delay, []).append(functools.partial(event, j))
            else:
                late.append((at + delay, functools.partial(event, j)))
    late.sort(key=lambda item: item[0])

    def at_sweep(T, table_of):
        for at, events in sorted(table_of.items()):

            @pl.when(T == at)
            def _():
                for event in events:
                    event()

    halo_wait(0)

    def sweep(T, carry):
        at_sweep(T, before)
        for n in range(1, STEPS + 1):
            t = T - (n - 1)
            high = tiles - 2 + p if n == STEPS else tiles - 1

            @pl.when((t >= 0) & (t <= high))
            def _():
                first_step(t) if n == 1 else later_step(n, t)

        at_sweep(T, after)
        return carry

    lax.fori_loop(0, sweeps, sweep, 0)
    for _, event in late:
        event()

    for j in range(len(out_chunks)):
        for here, there, back in fin_copies(j) + field_copies(j):
            here.wait()
            there.wait_send()
            back.wait_recv()
        near_copy(j).wait_send()
        for copy in far_copies(j):
            copy.wait_send()
    for copy in xc + xk + ag_z + [ag_pair]:
        copy.wait_send()
    for d in range(1, grid_y):
        y_each(py, lambda full: y_copy(d, py, full).wait_send())
    for c in range(len(in_chunks)):

        @pl.when(not_last)
        def _():
            for kind in range(2):
                z_copy(c, kind, True).wait_send()

        @pl.when(not_first)
        def _():
            for kind in range(2):
                z_copy(c, kind, False).wait_send()


def local(slabs, grid_y, grid_z, material, eps_table, surface_mask, excite_map, mode_profiles, port_eps, cotangent):
    tiles = slabs // 2 + 1
    height = 8 * tiles + 2 * PAD
    half, rows = 4 * slabs, 8 * slabs
    chunks, outs = len(cuts(tiles, (3, 3, 4, 4, 3))), len(cuts(tiles - 1, (6, 5, 3, 2)))
    vmem = lambda *shape: pltpu.VMEM(shape, F32)
    dma = lambda *shape: pltpu.SemaphoreType.DMA(shape)
    field = lambda layers: vmem(layers, 2, 2, height, 128)
    smem_spec = pl.BlockSpec(memory_space=pltpu.SMEM)
    vmem_spec = pl.BlockSpec(memory_space=pltpu.VMEM)
    any_spec = pl.BlockSpec(memory_space=pl.ANY)
    scratch = [
        vmem(LAYERS, 2, height, 128),
        vmem(LAYERS - 2, 2, height, 128),
        vmem(DEPTH, 2, height, 128),
        pltpu.VMEM((DEPTH, 2, rows, 128), jnp.int32),
        field(LAYERS - 2), field(LAYERS - 2), field(LAYERS - 2),
        field(LAYERS - 1), field(LAYERS - 1), field(LAYERS - 1),
        vmem(2 * DEPTH, 2, height, 128),
        vmem(STEPS, 2, height, 128),
        vmem(slabs, 4, 8, 128),
        vmem(2 * DEPTH, half, 128), vmem(2 * DEPTH, half, 128),
        vmem(DEPTH, half, 128), vmem(2, DEPTH, half, 128), vmem(DEPTH, rows, 128),
        dma(4), dma(grid_z + grid_y - 1), dma(grid_z + grid_y - 1),
        dma(chunks, 2), dma(chunks, 2), dma(chunks), dma(chunks), dma(2, 2, chunks), dma(2, 2, chunks),
        dma(outs), dma(outs), dma(3, outs), dma(3, outs),
        dma(2, outs), dma(2, outs), dma(2, outs), dma(2, outs), dma(2, outs), dma(2, outs),
    ]
    return pl.pallas_call(
        functools.partial(kernel, slabs, grid_y, grid_z),
        out_shape=(
            jax.ShapeDtypeStruct(material.shape, F32),
            jax.ShapeDtypeStruct(cotangent.shape, F32),
        ),
        in_specs=[smem_spec, smem_spec, smem_spec, vmem_spec, vmem_spec, any_spec, any_spec],
        out_specs=(any_spec, any_spec),
        scratch_shapes=scratch,
        compiler_params=pltpu.CompilerParams(
            collective_id=0, has_side_effects=True, vmem_limit_bytes=60 * 1024 * 1024
        ),
        cost_estimate=pl.CostEstimate(flops=600_000_000, bytes_accessed=6_000_000, transcendentals=0),
    )(eps_table, surface_mask, excite_map, mode_profiles, port_eps, material, cotangent)


def solution(mesh):
    slabs = mesh.shape["slab"]
    grid_z = 4 if slabs == 32 else 2
    grid_y = slabs // 2 // grid_z
    in_specs = (
        P("slab", None, None),
        P(),
        P("slab"),
        P("run"),
        P(None, "slab", None),
        P("slab", None),
        P("run", "slab", None, None),
    )
    out_specs = (P("slab", None, None), P("run", "slab", None, None))
    return jax.shard_map(
        functools.partial(local, slabs, grid_y, grid_z),
        mesh=mesh, in_specs=in_specs, out_specs=out_specs, check_vma=False,
    )
```

```python
import functools
import math

import jax
import jax.numpy as jnp
from jax import lax
from jax.experimental import pallas as pl
from jax.experimental.pallas import tpu as pltpu
from jax.sharding import PartitionSpec as P

STEPS = 6
F32 = jnp.float32
DEPTH = 4
LAYERS = 2 * DEPTH + 2 * STEPS
PAD = 8
FIRST = STEPS
IN_SIZES = (2, 3, 4, 4, 4)
OUT_SIZES = (4, 4, 4, 2, 2)
PASS_AT = (-1, -1, 0, 2, 5)


def forcing_of(n):
    t = float(n + 1)
    return 2.0 * math.sin(0.3 * t) * (1.0 - math.exp(-0.5 * t))


def cuts(total, sizes):
    spans, at = [], 0
    for size in sizes:
        if at < total:
            spans.append((at, min(total, at + size)))
            at += size
    if at < total:
        spans.append((at, total))
    return spans


def z_order(back):
    z = lax.broadcasted_iota(jnp.int32, (256, 256), 1 if back else 0)
    place = lax.broadcasted_iota(jnp.int32, (256, 256), 0 if back else 1)
    return (z == 2 * (place % 128) + place // 128).astype(F32).astype(jnp.bfloat16)


def reorder(v, order):
    high = v.astype(jnp.bfloat16)
    rest = v - high.astype(F32)
    middle = rest.astype(jnp.bfloat16)
    low = (rest - middle.astype(F32)).astype(jnp.bfloat16)
    dot = lambda part: jnp.dot(part, order, preferred_element_type=F32)
    return (dot(high) + dot(middle)) + dot(low)


def restore(grad_p, field_p, grad, field):
    order = z_order(True)
    grad[0] = reorder(jnp.concatenate([grad_p[0, 0], grad_p[0, 1]], 1), order)
    field[0, 0] = reorder(jnp.concatenate([field_p[0, 0], field_p[0, 1]], 1), order)


def kernel(
    slabs, grid_y, grid_z,
    eps_s, mask_s, excite_s, profiles_v, port_v, material_h, cot_h,
    grad_h, out_h,
    C, K, SC, SK, MT, CR, EX, EY, EZ, GX, GY, GZ, GR, W, gath, near, part, far, side, fin,
    load_sem, ag_send, ag_recv, xc_send, xc_recv, xk_send, xk_recv, z_send, z_recv, sib_send, sib_recv,
    near_send, near_recv, far_send, far_recv, fin_copy, fin_send, fin_recv, fo_copy, fo_send, fo_recv,
):
    half = 4 * slabs
    tiles = slabs // 2 + 1
    rows_all = 8 * tiles
    pairs = slabs // 2
    in_chunks = cuts(tiles, IN_SIZES)
    out_chunks = cuts(tiles - 1, OUT_SIZES)
    s = lax.axis_index("slab")
    r = lax.axis_index("run")
    p = lax.rem(s, 2)
    m = s // 2
    core = lax.rem(r, 2)
    other_core = r + 1 - 2 * core
    other_run = lax.rem(r + 2, 4)
    mate = s + 1 - 2 * p
    py, pz = m // grid_z, lax.rem(m, grid_z)
    not_first, not_last = m > 0, m < pairs - 1
    window = p * (slabs // 2 - 1)
    base, mate_base = 8 * window, 8 * ((1 - p) * (slabs // 2 - 1))
    own, mates = FIRST + DEPTH * p, FIRST + DEPTH * (1 - p)

    def to(slab, run):
        return {"slab": slab, "run": run}

    def remote(src, dst, send, recv, slab, run):
        return pltpu.make_async_remote_copy(
            src_ref=src, dst_ref=dst, send_sem=send, recv_sem=recv,
            device_id=to(slab, run), device_id_type=pl.DeviceIdType.MESH,
        )

    def ds8(start, size):
        return pl.ds(pl.multiple_of(start, 8), size)

    load_cot = pltpu.make_async_copy(cot_h.at[0], CR, load_sem.at[0])
    load_material = pltpu.make_async_copy(material_h, MT, load_sem.at[1])
    load_cot.start()
    load_material.start()

    z_mates = [(py * grid_z + lax.rem(pz + d, grid_z)) * 2 + p for d in range(1, grid_z)]
    y_mates = [(lax.rem(py + d, grid_y) * grid_z + pz) * 2 + p for d in range(1, grid_y)]
    barrier = pltpu.get_barrier_semaphore()

    def hello(slab, run):
        pl.semaphore_signal(barrier, inc=1, device_id=to(slab, run), device_id_type=pl.DeviceIdType.MESH)

    hello(mate, r)
    hello(mate, other_run)
    hello(s, other_core)
    hello(s, other_run)
    for peer in z_mates + y_mates:
        hello(peer, r)

    @pl.when(not_first)
    def _():
        hello(s - 2, r)

    @pl.when(not_last)
    def _():
        hello(s + 2, r)

    picked = jnp.zeros((8, 256), F32)
    for j in range(4):
        picked = jnp.where(excite_s[0] == j, profiles_v[j], picked)
    port = 0.25 / port_v[...]
    order = z_order(False)
    port_block = reorder(jnp.concatenate([picked, port], 0), order)
    for h in range(2):
        gath[s, h] = port_block[0:8, 128 * h : 128 * h + 128]
        gath[s, 2 + h] = port_block[8:16, 128 * h : 128 * h + 128]

    zero_row = jnp.zeros((8, 128), F32)
    bottom = jnp.zeros((2, 2, 8, 128), F32)

    def clear(i, carry):
        C[i, :, pl.ds(PAD + rows_all, 8), :] = jnp.zeros((2, 8, 128), F32)
        return carry

    lax.fori_loop(0, LAYERS, clear, 0)

    def clear_fields(i, carry):
        EX[i, :, :, pl.ds(PAD + rows_all, 8), :] = bottom
        EZ[i, :, :, pl.ds(PAD + rows_all, 8), :] = bottom
        GX[i, :, :, pl.ds(0, 8), :] = bottom
        GZ[i, :, :, pl.ds(0, 8), :] = bottom
        return carry

    lax.fori_loop(0, LAYERS - 2, clear_fields, 0)
    GX[LAYERS - 2, :, :, pl.ds(0, 8), :] = bottom
    GZ[LAYERS - 2, :, :, pl.ds(0, 8), :] = bottom
    for n in range(STEPS):
        for edge in (0, PAD + rows_all):
            W[n, :, pl.ds(edge, 8), :] = jnp.zeros((2, 8, 128), F32)

    def clear_end(c_first, k_first):
        def one(t, carry):
            rows = ds8(8 * t, 8)
            C[pl.ds(c_first, STEPS), :, rows, :] = jnp.zeros((STEPS, 2, 8, 128), F32)
            K[pl.ds(k_first, STEPS - 1), :, rows, :] = jnp.zeros((STEPS - 1, 2, 8, 128), F32)
            return carry

        lax.fori_loop(0, tiles + 1, one, 0)

    @pl.when(m == 0)
    def _():
        clear_end(0, 0)

    @pl.when(m == pairs - 1)
    def _():
        clear_end(FIRST + 2 * DEPTH, FIRST + 2 * DEPTH - 1)

    def k_rows(c):
        start, stop = in_chunks[c]
        first = 0 if c == 0 else PAD + 8 * start
        return pl.ds(first, PAD + 8 * stop - first)

    def c_rows(c):
        start, stop = in_chunks[c]
        return pl.ds(PAD + 8 * start, 8 * (stop - start))

    for j in range(DEPTH):
        tile = jnp.full((8, 128), mask_s[j].astype(F32), F32)
        SK[j, pl.ds(0, 8), :] = tile
        for h in range(2):
            K[own - 1 + j, h, pl.ds(0, 8), :] = tile

    pl.semaphore_wait(
        barrier, 4 + (grid_z - 1) + (grid_y - 1) + not_first.astype(jnp.int32) + not_last.astype(jnp.int32)
    )

    ag_pair = remote(gath.at[s], gath.at[s], ag_send.at[0], ag_recv.at[0], mate, r)
    ag_pair.start()

    def cot_rows(c, first):
        start, stop = in_chunks[c]
        size = 8 * (stop - start)
        v = CR[:, ds8(first + 8 * start, size), :].reshape(DEPTH * size, 256)
        return reorder(v, order).reshape(DEPTH, size, 256)

    load_cot.wait()
    xc = []
    for c in range(len(in_chunks)):
        v = cot_rows(c, mate_base)
        for h in range(2):
            SC[:, h, c_rows(c), :] = v[:, :, 128 * h : 128 * h + 128]
        copy = remote(
            SC.at[:, :, c_rows(c), :], C.at[pl.ds(own, DEPTH), :, c_rows(c), :], xc_send.at[c], xc_recv.at[c], mate, r
        )
        copy.start()
        xc.append(copy)

    table = [0.25 / jnp.full((1, 8, 128), eps_s[j], F32) for j in range(16)]

    def coefficient_of(index):
        rows = index.shape[1] // 8
        level = [jnp.concatenate([entry] * rows, 1) for entry in table]
        for bit in range(4):
            odd = ((index >> bit) & 1) != 0
            level = [jnp.where(odd, level[2 * j + 1], level[2 * j]) for j in range(len(level) // 2)]
        return level[0]

    def material_rows(c, first):
        start, stop = in_chunks[c]
        size = 8 * (stop - start)
        v = MT[:, ds8(first + 8 * start, size), :].reshape(DEPTH * size, 256).astype(F32).astype(jnp.bfloat16)
        return jnp.dot(v, order, preferred_element_type=F32).reshape(DEPTH, size, 256)

    load_material.wait()
    xk = []
    for c in range(len(in_chunks)):
        v = material_rows(c, mate_base)
        v = jnp.where(core == 0, v[:, :, :128], v[:, :, 128:])
        SK[:, c_rows(c), :] = coefficient_of(v.astype(jnp.int32))
        copy = remote(
            SK.at[:, k_rows(c), :], K.at[pl.ds(own - 1, DEPTH), core, k_rows(c), :],
            xk_send.at[c], xk_recv.at[c], mate, other_run,
        )
        copy.start()
        xk.append(copy)
    for c in range(len(in_chunks)):
        v = cot_rows(c, base)
        index = material_rows(c, base).astype(jnp.int32)
        for h in range(2):
            C[pl.ds(own, DEPTH), h, c_rows(c), :] = v[:, :, 128 * h : 128 * h + 128]
            K[pl.ds(own - 1, DEPTH), h, c_rows(c), :] = coefficient_of(index[:, :, 128 * h : 128 * h + 128])

    remote(gath.at[mate], gath.at[mate], ag_send.at[0], ag_recv.at[0], mate, r).wait_recv()
    ag_z = []
    for d in range(1, grid_z):
        copy = remote(
            gath.at[pl.ds(2 * m, 2)], gath.at[pl.ds(2 * m, 2)], ag_send.at[d], ag_recv.at[d], z_mates[d - 1], r
        )
        copy.start()
        ag_z.append(copy)

    def z_copy(c, kind, up):
        way = 0 if up else 1
        target = s + 2 if up else s - 2
        if kind == 0:
            src, dst = (FIRST + 2, 0) if up else (FIRST, FIRST + 2 * DEPTH)
            src_ref = C.at[pl.ds(src, STEPS), :, c_rows(c), :]
            dst_ref = C.at[pl.ds(dst, STEPS), :, c_rows(c), :]
        else:
            src, dst = (FIRST + 2, 0) if up else (FIRST - 1, FIRST + 2 * DEPTH - 1)
            src_ref = K.at[pl.ds(src, STEPS - 1), core, k_rows(c), :]
            dst_ref = K.at[pl.ds(dst, STEPS - 1), core, k_rows(c), :]
        return remote(src_ref, dst_ref, z_send.at[way, kind, c], z_recv.at[way, kind, c], target, r)

    def share(c, part, h):
        first, size = ((mates - 1, DEPTH), (0, STEPS - 1), (FIRST + 2 * DEPTH - 1, STEPS - 1))[part]
        ref = K.at[pl.ds(first, size), h, k_rows(c), :]
        return remote(ref, ref, sib_send.at[part, c], sib_recv.at[part, c], s, other_core)

    def pass_on(c):
        remote(
            SK.at[:, k_rows(c), :], K.at[pl.ds(mates - 1, DEPTH), core, k_rows(c), :],
            xk_send.at[c], xk_recv.at[c], mate, other_run,
        ).wait_recv()
        remote(
            SC.at[:, :, c_rows(c), :], C.at[pl.ds(mates, DEPTH), :, c_rows(c), :],
            xc_send.at[c], xc_recv.at[c], mate, r,
        ).wait_recv()

        @pl.when(not_last)
        def _():
            for kind in (1, 0):
                z_copy(c, kind, True).start()

        @pl.when(not_first)
        def _():
            for kind in (1, 0):
                z_copy(c, kind, False).start()

        share(c, 0, core).start()

    def pass_across(c):
        @pl.when(not_first)
        def _():
            z_copy(c, 1, True).wait_recv()
            share(c, 1, core).start()

        @pl.when(not_last)
        def _():
            z_copy(c, 1, False).wait_recv()
            share(c, 2, core).start()

    def halo_wait(c):
        share(c, 0, 1 - core).wait_recv()

        @pl.when(not_first)
        def _():
            z_copy(c, 0, True).wait_recv()
            share(c, 1, 1 - core).wait_recv()

        @pl.when(not_last)
        def _():
            z_copy(c, 0, False).wait_recv()
            share(c, 2, 1 - core).wait_recv()

    pass_on(0)

    for d in range(1, grid_z):
        source = (py * grid_z + lax.rem(pz - d + grid_z, grid_z)) * 2
        remote(
            gath.at[pl.ds(source, 2)], gath.at[pl.ds(source, 2)], ag_send.at[d], ag_recv.at[d], z_mates[d - 1], r
        ).wait_recv()

    group = 2 * grid_z

    def whole(y):
        return jnp.where(p == 0, y < grid_y // 2, y >= grid_y // 2)

    def single(y):
        return y == grid_y // 2 - p

    single_slot = slabs // 2 - p

    def y_copy(d, y, full):
        slots = pl.ds(group * y, group) if full else pl.ds(single_slot, 1)
        return remote(
            gath.at[slots], gath.at[slots], ag_send.at[grid_z + d - 1], ag_recv.at[grid_z + d - 1], y_mates[d - 1], r
        )

    def y_each(y, action):
        @pl.when(whole(y))
        def _():
            action(True)

        @pl.when(single(y))
        def _():
            action(False)

    for d in range(1, grid_y):
        y_each(py, lambda full: y_copy(d, py, full).start())
    for c in range(1, len(in_chunks)):
        if PASS_AT[c] < 0:
            pass_on(c)
    for d in range(1, grid_y):
        source = lax.rem(py - d + grid_y, grid_y)
        y_each(source, lambda full: y_copy(d, source, full).wait_recv())

    lane = lax.broadcasted_iota(jnp.int32, (1, 1, 8, 128), 3)
    is_last, is_first = lane == 127, lane == 0

    def up_z(v):
        turned = pltpu.roll(v[0:1], 127, v.ndim - 1)
        turned = jnp.where(is_last if v.ndim == 4 else is_last[0], 0.0, turned)
        return jnp.concatenate([v[1:2], turned], 0)

    def down_z(v):
        turned = pltpu.roll(v[1:2], 1, v.ndim - 1)
        turned = jnp.where(is_first if v.ndim == 4 else is_first[0], 0.0, turned)
        return jnp.concatenate([turned, v[0:1]], 0)

    inside = not_first.astype(F32)

    def source_of(n, t, rows, ahead_rows, behind_rows):
        slot = window + t
        drive = (0.5 * forcing_of(n - 1)) * gath[slot, pl.ds(0, 2)]
        if n == 1:
            W[0, :, rows, :] = drive
            return drive, drive
        now = W[n - 2, :, rows, :]
        around = W[n - 2, :, ahead_rows, :] + W[n - 2, :, behind_rows, :] + up_z(now) + down_z(now)
        value = 2.0 * now + gath[slot, pl.ds(2, 2)] * (around - 4.0 * now) + drive
        if n > 2:
            value = value - W[n - 3, :, rows, :]
        W[n - 1, :, rows, :] = value
        return value, value - now

    def add_driven(v, extra):
        return jnp.concatenate([v[:, 0:1] + extra[:, None], v[:, 1:2]], 1)

    def product(a):
        return a[:, 0] * a[:, 1]

    def first_step(t):
        rows = ds8(PAD + 8 * t, 8)
        ahead_rows, behind_rows = pl.ds(PAD + 8 * t + 1, 8), pl.ds(PAD + 8 * t - 1, 8)
        ie, ih = source_of(1, t, rows, ahead_rows, behind_rows)
        zero = jnp.zeros((2, 8, 128), F32)
        both = lambda d, e: jnp.stack([d, e], 1)
        follow = C[0, :, rows, :]
        gx_l = gy_l = gyd_l = None
        for i in range(LAYERS - 1):
            c = follow
            follow = C[i + 1, :, rows, :]
            gx = c - C[i, :, ahead_rows, :]
            gy = follow - c
            gyd = c - up_z(c)
            GX[i, :, :, rows, :] = both(zero, gx)
            GY[i, :, :, rows, :] = both(gyd, gy)
            GZ[i, :, :, rows, :] = both(-gx, zero)
            if i >= 1:
                if i == FIRST:
                    gx_l, gy_l, gyd_l = gx_l * inside, gy_l * inside, gyd_l * inside
                k = K[i - 1, :, rows, :]
                mask = K[i - 1, 0:1, pl.ds(0, 8), :]
                gx_y = gx - GX[i, :, 1, behind_rows, :]
                ex_d = c - k * (gx_y + (gyd - down_z(gyd)))
                ey_d = k * ((gx - gx_l) + mask * ih)
                ez_d = k * ((gyd - gyd_l) + mask * ie)
                ex_s = k * (down_z(gy) - gy)
                ey_s = k * (gx - down_z(gx))
                ez_s = c + k * ((gy - gy_l) - gx_y)
                EX[i - 1, :, :, rows, :] = both(ex_d, ex_s)
                EY[i - 1, :, :, rows, :] = both(ey_d, ey_s)
                EZ[i - 1, :, :, rows, :] = both(ez_d, ez_s)
                if FIRST <= i < FIRST + 2 * DEPTH:
                    GR[i - FIRST, :, rows, :] = ex_d * ex_s + ey_d * ey_s + ez_d * ez_s
            gx_l, gy_l, gyd_l = gx, gy, gyd

    def later_step(n, t):
        rows = ds8(PAD + 8 * t, 8)
        ahead_rows, behind_rows = pl.ds(PAD + 8 * t + 1, 8), pl.ds(PAD + 8 * t - 1, 8)
        ie, ih = source_of(n, t, rows, ahead_rows, behind_rows)
        ey_n, ez_n = EY[n - 2, :, :, rows, :], EZ[n - 2, :, :, rows, :]
        gy_l = gz_l = None
        for i in range(n - 1, LAYERS - n):
            ex, ey, ez = EX[i - 1, :, :, rows, :], ey_n, ez_n
            ey_n, ez_n = EY[i, :, :, rows, :], EZ[i, :, :, rows, :]
            gx = GX[i, :, :, rows, :] + ((ez - EZ[i - 1, :, :, ahead_rows, :]) + (up_z(ey) - ey))
            gy = GY[i, :, :, rows, :] + ((ex - up_z(ex)) + (ez_n - ez))
            gz = GZ[i, :, :, rows, :] + ((ey - ey_n) + (EX[i - 1, :, :, ahead_rows, :] - ex))
            GX[i, :, :, rows, :] = gx
            GY[i, :, :, rows, :] = gy
            GZ[i, :, :, rows, :] = gz
            if i >= n:
                if i == FIRST:
                    gy_l, gz_l = gy_l * inside, gz_l * inside
                k = K[i - 1, :, rows, :][:, None]
                mask = K[i - 1, 0:1, pl.ds(0, 8), :]
                ex = ex + k * ((gz - GZ[i, :, :, behind_rows, :]) - (gy - down_z(gy)))
                ey = ey + k * add_driven((gx - down_z(gx)) - (gz - gz_l), mask * ih)
                ez = ez + k * add_driven((gy - gy_l) - (gx - GX[i, :, :, behind_rows, :]), mask * ie)
                EX[i - 1, :, :, rows, :] = ex
                EY[i - 1, :, :, rows, :] = ey
                EZ[i - 1, :, :, rows, :] = ez
                if FIRST <= i < FIRST + 2 * DEPTH:
                    GR[i - FIRST, :, rows, :] = GR[i - FIRST, :, rows, :] + (product(ex) + product(ey) + product(ez))
            gy_l, gz_l = gy, gz

    def near_copy(j):
        first, stop = out_chunks[j]
        return remote(
            GR.at[:, 1 - core, ds8(PAD + 8 * (p + first), 8 * (stop - first)), :],
            near.at[:, pl.ds(8 * first, 8 * (stop - first)), :],
            near_send.at[j], near_recv.at[j], s, other_core,
        )

    def far_copies(j):
        first, stop = out_chunks[j]
        rows = pl.ds(8 * first, 8 * (stop - first))
        mine, theirs = pl.ds(DEPTH * p, DEPTH), pl.ds(DEPTH * (1 - p), DEPTH)
        return [
            remote(part.at[mine, rows, :], far.at[:, rows, :], far_send.at[0, j], far_recv.at[0, j], s, other_run),
            remote(part.at[theirs, rows, :], side.at[0, :, rows, :], far_send.at[1, j], far_recv.at[1, j], mate, r),
            remote(
                part.at[theirs, rows, :], side.at[1, :, rows, :], far_send.at[2, j], far_recv.at[2, j], mate, other_run
            ),
        ]

    def fin_copies(j):
        first, stop = out_chunks[j]
        copies = []
        for k in range(2):
            rows = ds8(half * k + 8 * first, 8 * (stop - first))
            src = fin.at[:, rows, :]
            dst = grad_h.at[:, core, rows, :]
            copies.append(
                (
                    pltpu.make_async_copy(src, dst, fin_copy.at[k, j]),
                    remote(src, dst, fin_send.at[k, j], fin_recv.at[k, j], s, other_core),
                    remote(
                        src, grad_h.at[:, 1 - core, rows, :],
                        fin_send.at[k, j], fin_recv.at[k, j], s, other_core,
                    ),
                )
            )
        return copies

    def field_copies(j):
        first, stop = out_chunks[j]
        size = 8 * (stop - first)
        src_rows = ds8(PAD + 8 * (p + first), size)
        dst = out_h.at[:, :, ds8(half * p + 8 * first, size), :]
        back = out_h.at[:, :, ds8(half * (1 - p) + 8 * first, size), :]
        src = EY.at[pl.ds(mates - 1, DEPTH), :, 0, src_rows, :]
        return [
            (
                pltpu.make_async_copy(EY.at[pl.ds(own - 1, DEPTH), :, 0, src_rows, :], dst, fo_copy.at[j]),
                remote(src, dst, fo_send.at[j], fo_recv.at[j], mate, r),
                remote(src, back, fo_send.at[j], fo_recv.at[j], mate, r),
            )
        ]

    def rows_done(j):
        near_copy(j).start()
        for here, there, _ in field_copies(j):
            there.start()
            here.start()

    def sum_cores(j):
        first, stop = out_chunks[j]
        near_copy(j).wait_recv()

        def one(t, carry):
            rows = ds8(8 * t, 8)
            part[:, rows, :] = GR[:, core, ds8(PAD + 8 * (p + t), 8), :] + near[:, rows, :]
            return carry

        lax.fori_loop(first, stop, one, 0)
        for copy in far_copies(j):
            copy.start()

    def sum_chips(j):
        first, stop = out_chunks[j]
        for copy in far_copies(j):
            copy.wait_recv()

        def one(t, carry):
            rows = ds8(8 * t, 8)
            fin[:, ds8(half * p + 8 * t, 8), :] = part[pl.ds(DEPTH * p, DEPTH), rows, :] + far[:, rows, :]
            fin[:, ds8(half * (1 - p) + 8 * t, 8), :] = side[0, :, rows, :] + side[1, :, rows, :]
            return carry

        lax.fori_loop(first, stop, one, 0)
        for here, there, _ in fin_copies(j):
            there.start()
            here.start()

    sweeps = tiles + STEPS - 1
    before, after, late = {}, {}, []
    for c in range(1, len(in_chunks)):
        at = in_chunks[c][0] - 1
        if PASS_AT[c] >= 0:
            before.setdefault(PASS_AT[c], []).append(functools.partial(pass_on, c))
        before.setdefault(max(0, at - 2), []).append(functools.partial(pass_across, c))
        before.setdefault(at, []).append(functools.partial(halo_wait, c))
    for j in range(len(out_chunks)):
        at = out_chunks[j][1] + STEPS - 1
        for event, delay in ((rows_done, 0), (sum_cores, 2), (sum_chips, 5)):
            if at + delay < sweeps:
                after.setdefault(at + delay, []).append(functools.partial(event, j))
            else:
                late.append((at + delay, functools.partial(event, j)))
    late.sort(key=lambda item: item[0])

    def at_sweep(T, table_of):
        for at, events in sorted(table_of.items()):

            @pl.when(T == at)
            def _():
                for event in events:
                    event()

    pass_across(0)
    halo_wait(0)

    def sweep(T, carry):
        at_sweep(T, before)
        for n in range(1, STEPS + 1):
            t = T - (n - 1)
            high = tiles - 2 + p if n == STEPS else tiles - 1

            @pl.when((t >= 0) & (t <= high))
            def _():
                first_step(t) if n == 1 else later_step(n, t)

        at_sweep(T, after)
        return carry

    lax.fori_loop(0, sweeps, sweep, 0)
    for _, event in late:
        event()

    for j in range(len(out_chunks)):
        for here, there, back in fin_copies(j) + field_copies(j):
            here.wait()
            there.wait_send()
            back.wait_recv()
        near_copy(j).wait_send()
        for copy in far_copies(j):
            copy.wait_send()
    for copy in xc + xk + ag_z + [ag_pair]:
        copy.wait_send()
    for d in range(1, grid_y):
        y_each(py, lambda full: y_copy(d, py, full).wait_send())
    for c in range(len(in_chunks)):
        share(c, 0, core).wait_send()

        @pl.when(not_last)
        def _():
            share(c, 2, core).wait_send()
            for kind in range(2):
                z_copy(c, kind, True).wait_send()

        @pl.when(not_first)
        def _():
            share(c, 1, core).wait_send()
            for kind in range(2):
                z_copy(c, kind, False).wait_send()


def local(slabs, grid_y, grid_z, material, eps_table, surface_mask, excite_map, mode_profiles, port_eps, cotangent):
    tiles = slabs // 2 + 1
    height = 8 * tiles + 2 * PAD
    half, rows = 4 * slabs, 8 * slabs
    chunks, outs = len(cuts(tiles, IN_SIZES)), len(cuts(tiles - 1, OUT_SIZES))
    vmem = lambda *shape: pltpu.VMEM(shape, F32)
    dma = lambda *shape: pltpu.SemaphoreType.DMA(shape)
    field = lambda layers: vmem(layers, 2, 2, height, 128)
    smem_spec = pl.BlockSpec(memory_space=pltpu.SMEM)
    vmem_spec = pl.BlockSpec(memory_space=pltpu.VMEM)
    any_spec = pl.BlockSpec(memory_space=pl.ANY)
    scratch = [
        vmem(LAYERS, 2, height, 128),
        vmem(LAYERS - 2, 2, height, 128),
        vmem(DEPTH, 2, height, 128),
        vmem(DEPTH, height, 128),
        pltpu.VMEM((DEPTH, rows, 256), jnp.int32),
        vmem(DEPTH, rows, 256),
        field(LAYERS - 2), field(LAYERS - 2), field(LAYERS - 2),
        field(LAYERS - 1), field(LAYERS - 1), field(LAYERS - 1),
        vmem(2 * DEPTH, 2, height, 128),
        vmem(STEPS, 2, height, 128),
        vmem(slabs, 4, 8, 128),
        vmem(2 * DEPTH, half, 128), vmem(2 * DEPTH, half, 128),
        vmem(DEPTH, half, 128), vmem(2, DEPTH, half, 128), vmem(DEPTH, rows, 128),
        dma(2), dma(grid_z + grid_y - 1), dma(grid_z + grid_y - 1),
        dma(chunks), dma(chunks), dma(chunks), dma(chunks), dma(2, 2, chunks), dma(2, 2, chunks),
        dma(3, chunks), dma(3, chunks),
        dma(outs), dma(outs), dma(3, outs), dma(3, outs),
        dma(2, outs), dma(2, outs), dma(2, outs), dma(outs), dma(outs), dma(outs),
    ]
    split = jax.ShapeDtypeStruct((DEPTH, 2, rows, 128), F32)
    grad_p, field_p = pl.pallas_call(
        functools.partial(kernel, slabs, grid_y, grid_z),
        out_shape=(split, split),
        in_specs=[smem_spec, smem_spec, smem_spec, vmem_spec, vmem_spec, any_spec, any_spec],
        out_specs=(any_spec, any_spec),
        scratch_shapes=scratch,
        compiler_params=pltpu.CompilerParams(
            collective_id=0, has_side_effects=True, vmem_limit_bytes=60 * 1024 * 1024
        ),
        cost_estimate=pl.CostEstimate(flops=600_000_000, bytes_accessed=6_000_000, transcendentals=0),
    )(eps_table, surface_mask, excite_map, mode_profiles, port_eps, material, cotangent)
    halves = pl.BlockSpec((1, 2, rows, 128), lambda x: (x, 0, 0, 0))
    return pl.pallas_call(
        restore,
        grid=(DEPTH,),
        out_shape=(
            jax.ShapeDtypeStruct(material.shape, F32),
            jax.ShapeDtypeStruct(cotangent.shape, F32),
        ),
        in_specs=[halves, halves],
        out_specs=(
            pl.BlockSpec((1, rows, 256), lambda x: (x, 0, 0)),
            pl.BlockSpec((1, 1, rows, 256), lambda x: (0, x, 0, 0)),
        ),
        compiler_params=pltpu.CompilerParams(vmem_limit_bytes=60 * 1024 * 1024),
    )(grad_p, field_p)


def solution(mesh):
    slabs = mesh.shape["slab"]
    grid_z = 4 if slabs == 32 else 2
    grid_y = slabs // 2 // grid_z
    in_specs = (
        P("slab", None, None),
        P(),
        P("slab"),
        P("run"),
        P(None, "slab", None),
        P("slab", None),
        P("run", "slab", None, None),
    )
    out_specs = (P("slab", None, None), P("run", "slab", None, None))
    return jax.shard_map(
        functools.partial(local, slabs, grid_y, grid_z),
        mesh=mesh, in_specs=in_specs, out_specs=out_specs, check_vma=False,
    )
```

```python
import functools
import math

import jax
import jax.numpy as jnp
from jax import lax
from jax.experimental import pallas as pl
from jax.experimental.pallas import tpu as pltpu
from jax.sharding import PartitionSpec as P

STEPS = 6
F32 = jnp.float32
DEPTH = 4
LAYERS = 2 * DEPTH + 2 * STEPS
PAD = 8
FIRST = STEPS
IN_SIZES = (2, 3, 4, 4, 4)
OUT_SIZES = (2, 2, 3, 3, 3, 2, 1)
PASS_AT = (-1, -1, 0, 2, 5)


def forcing_of(n):
    t = float(n + 1)
    return 2.0 * math.sin(0.3 * t) * (1.0 - math.exp(-0.5 * t))


def cuts(total, sizes):
    spans, at = [], 0
    for size in sizes:
        if at < total:
            spans.append((at, min(total, at + size)))
            at += size
    if at < total:
        spans.append((at, total))
    return spans


def z_order(back):
    z = lax.broadcasted_iota(jnp.int32, (256, 256), 1 if back else 0)
    place = lax.broadcasted_iota(jnp.int32, (256, 256), 0 if back else 1)
    return (z == 2 * (place % 128) + place // 128).astype(F32).astype(jnp.bfloat16)


def reorder(v, order):
    high = v.astype(jnp.bfloat16)
    rest = v - high.astype(F32)
    middle = rest.astype(jnp.bfloat16)
    dot = lambda part: jnp.dot(part, order, preferred_element_type=F32)
    return dot(high) + dot(middle)


def restore(grad_p, field_p, grad, field):
    order = z_order(True)
    grad[0] = reorder(jnp.concatenate([grad_p[0, 0], grad_p[0, 1]], 1), order)
    field[0, 0] = reorder(jnp.concatenate([field_p[0, 0], field_p[0, 1]], 1), order)


def kernel(
    slabs, grid_y, grid_z,
    eps_s, mask_s, excite_s, profiles_v, port_v, material_h, cot_h,
    grad_h, out_h,
    C, K, SC, SK, MT, CR, EX, EY, EZ, GX, GY, GZ, GR, W, gath, near, part, far, side, fin,
    load_sem, port_send, port_recv, xc_send, xc_recv, xk_send, xk_recv, z_send, z_recv, sib_send, sib_recv,
    near_send, near_recv, far_send, far_recv, fin_copy, fin_send, fin_recv, fo_copy, fo_send, fo_recv,
):
    half = 4 * slabs
    tiles = slabs // 2 + 1
    rows_all = 8 * tiles
    pairs = slabs // 2
    in_chunks = cuts(tiles, IN_SIZES)
    out_chunks = cuts(tiles - 1, OUT_SIZES)
    s = lax.axis_index("slab")
    r = lax.axis_index("run")
    p = lax.rem(s, 2)
    m = s // 2
    core = lax.rem(r, 2)
    other_core = r + 1 - 2 * core
    other_run = lax.rem(r + 2, 4)
    mate = s + 1 - 2 * p
    py, pz = m // grid_z, lax.rem(m, grid_z)
    not_first, not_last = m > 0, m < pairs - 1
    window = p * (slabs // 2 - 1)
    base, mate_base = 8 * window, 8 * ((1 - p) * (slabs // 2 - 1))
    own, mates = FIRST + DEPTH * p, FIRST + DEPTH * (1 - p)

    def to(slab, run):
        return {"slab": slab, "run": run}

    def remote(src, dst, send, recv, slab, run):
        return pltpu.make_async_remote_copy(
            src_ref=src, dst_ref=dst, send_sem=send, recv_sem=recv,
            device_id=to(slab, run), device_id_type=pl.DeviceIdType.MESH,
        )

    def ds8(start, size):
        return pl.ds(pl.multiple_of(start, 8), size)

    load_cot = pltpu.make_async_copy(cot_h.at[0], CR, load_sem.at[0])
    load_material = pltpu.make_async_copy(material_h, MT, load_sem.at[1])
    load_cot.start()
    load_material.start()

    z_mates = [(py * grid_z + lax.rem(pz + d, grid_z)) * 2 + p for d in range(1, grid_z)]
    y_mates = [(lax.rem(py + d, grid_y) * grid_z + pz) * 2 + p for d in range(1, grid_y)]
    barrier = pltpu.get_barrier_semaphore()

    def hello(slab, run):
        pl.semaphore_signal(barrier, inc=1, device_id=to(slab, run), device_id_type=pl.DeviceIdType.MESH)

    hello(mate, r)
    hello(mate, other_run)
    hello(s, other_core)
    hello(s, other_run)

    for peer in z_mates + y_mates:
        hello(peer, r)

    @pl.when(not_first)
    def _():
        hello(s - 2, r)

    @pl.when(not_last)
    def _():
        hello(s + 2, r)

    picked = jnp.zeros((8, 256), F32)
    for j in range(4):
        picked = jnp.where(excite_s[0] == j, profiles_v[j], picked)
    port = 0.25 / port_v[...]
    order = z_order(False)
    port_block = reorder(jnp.concatenate([picked, port], 0), order)
    for h in range(2):
        gath[py, 2 * pz + p, h] = port_block[0:8, 128 * h : 128 * h + 128]
        gath[py, 2 * pz + p, 2 + h] = port_block[8:16, 128 * h : 128 * h + 128]

    zero_row = jnp.zeros((8, 128), F32)
    bottom = jnp.zeros((2, 2, 8, 128), F32)

    def clear(i, carry):
        C[i, :, pl.ds(PAD + rows_all, 8), :] = jnp.zeros((2, 8, 128), F32)
        return carry

    lax.fori_loop(0, LAYERS, clear, 0)

    def clear_fields(i, carry):
        EX[i, :, :, pl.ds(PAD + rows_all, 8), :] = bottom
        EZ[i, :, :, pl.ds(PAD + rows_all, 8), :] = bottom
        GX[i, :, :, pl.ds(0, 8), :] = bottom
        GZ[i, :, :, pl.ds(0, 8), :] = bottom
        return carry

    lax.fori_loop(0, LAYERS - 2, clear_fields, 0)
    GX[LAYERS - 2, :, :, pl.ds(0, 8), :] = bottom
    GZ[LAYERS - 2, :, :, pl.ds(0, 8), :] = bottom
    for n in range(STEPS):
        for edge in (0, PAD + rows_all):
            W[n, :, pl.ds(edge, 8), :] = jnp.zeros((2, 8, 128), F32)

    def clear_end(c_first, k_first):
        def one(t, carry):
            rows = ds8(8 * t, 8)
            C[pl.ds(c_first, STEPS), :, rows, :] = jnp.zeros((STEPS, 2, 8, 128), F32)
            K[pl.ds(k_first, STEPS - 1), :, rows, :] = jnp.zeros((STEPS - 1, 2, 8, 128), F32)
            return carry

        lax.fori_loop(0, tiles + 1, one, 0)

    @pl.when(m == 0)
    def _():
        clear_end(0, 0)

    @pl.when(m == pairs - 1)
    def _():
        clear_end(FIRST + 2 * DEPTH, FIRST + 2 * DEPTH - 1)

    def k_rows(c):
        start, stop = in_chunks[c]
        first = 0 if c == 0 else PAD + 8 * start
        return pl.ds(first, PAD + 8 * stop - first)

    def c_rows(c):
        start, stop = in_chunks[c]
        return pl.ds(PAD + 8 * start, 8 * (stop - start))

    for j in range(DEPTH):
        tile = jnp.full((8, 128), mask_s[j].astype(F32), F32)
        SK[j, pl.ds(0, 8), :] = tile
        for h in range(2):
            K[own - 1 + j, h, pl.ds(0, 8), :] = tile

    column = 2 * pz + p
    band = grid_y // 2

    def y_rows(d, y):
        rows = gath.at[y, column]
        return remote(rows, rows, port_send.at[d - 1], port_recv.at[d - 1], y_mates[d - 1], r)

    def mate_rows(place):
        rows = gath.at[:, place]
        return remote(rows, rows, port_send.at[grid_y - 1], port_recv.at[grid_y - 1], mate, r)

    def z_rows(d, z):
        rows = gath.at[pl.ds(band * p, band), pl.ds(2 * z, 2)]
        k = grid_y + d - 1
        return remote(rows, rows, port_send.at[k], port_recv.at[k], z_mates[d - 1], r)

    def edge_rows(d):
        rows = gath.at[band - p, (2 * grid_z - 1) * p]
        k = grid_y + grid_z + d - 2
        return remote(rows, rows, port_send.at[k], port_recv.at[k], z_mates[d - 1], r)

    def at_edge(z):
        return z == (grid_z - 1) * p

    def port_to_mate():
        for d in range(1, grid_y):
            y_rows(d, lax.rem(py - d + grid_y, grid_y)).wait_recv()
        mate_rows(column).start()

    def port_along_z():
        mate_rows(2 * pz + 1 - p).wait_recv()
        for d in range(1, grid_z):
            z_rows(d, pz).start()

        @pl.when(at_edge(pz))
        def _():
            for d in range(1, grid_z):
                edge_rows(d).start()

    def port_wait():
        for d in range(1, grid_z):
            source = lax.rem(pz - d + grid_z, grid_z)
            z_rows(d, source).wait_recv()

            @pl.when(at_edge(source))
            def _():
                edge_rows(d).wait_recv()

    def cot_rows(c, first):
        start, stop = in_chunks[c]
        size = 8 * (stop - start)
        v = CR[:, ds8(first + 8 * start, size), :].reshape(DEPTH * size, 256)
        return reorder(v, order).reshape(DEPTH, size, 256)

    table = [0.25 / jnp.full((1, 8, 128), eps_s[j], F32) for j in range(16)]

    def coefficient_of(index):
        rows = index.shape[1] // 8
        level = [jnp.concatenate([entry] * rows, 1) for entry in table]
        for bit in range(4):
            odd = ((index >> bit) & 1) != 0
            level = [jnp.where(odd, level[2 * j + 1], level[2 * j]) for j in range(len(level) // 2)]
        return level[0]

    def material_rows(c, first):
        start, stop = in_chunks[c]
        size = 8 * (stop - start)
        v = MT[:, ds8(first + 8 * start, size), :].reshape(DEPTH * size, 256).astype(F32).astype(jnp.bfloat16)
        return jnp.dot(v, order, preferred_element_type=F32).reshape(DEPTH, size, 256)

    def fill_mates(c):
        v = cot_rows(c, mate_base)
        for h in range(2):
            SC[:, h, c_rows(c), :] = v[:, :, 128 * h : 128 * h + 128]
        v = material_rows(c, mate_base)
        v = jnp.where(core == 0, v[:, :, :128], v[:, :, 128:])
        SK[:, c_rows(c), :] = coefficient_of(v.astype(jnp.int32))

    def fill_own(c):
        v = cot_rows(c, base)
        index = material_rows(c, base).astype(jnp.int32)
        for h in range(2):
            C[pl.ds(own, DEPTH), h, c_rows(c), :] = v[:, :, 128 * h : 128 * h + 128]
            K[pl.ds(own - 1, DEPTH), h, c_rows(c), :] = coefficient_of(index[:, :, 128 * h : 128 * h + 128])

    def x_copies(c):
        return [
            remote(
                SC.at[:, :, c_rows(c), :], C.at[pl.ds(own, DEPTH), :, c_rows(c), :], xc_send.at[c], xc_recv.at[c], mate, r
            ),
            remote(
                SK.at[:, k_rows(c), :], K.at[pl.ds(own - 1, DEPTH), core, k_rows(c), :],
                xk_send.at[c], xk_recv.at[c], mate, other_run,
            ),
        ]

    def z_copy(c, kind, up, part):
        way = 0 if up else 1
        target = s + 2 if up else s - 2
        middle = FIRST + DEPTH
        low, high = (FIRST + 2, FIRST + 2 * DEPTH) if up else (FIRST, FIRST + STEPS)
        shift = -2 * DEPTH if up else 2 * DEPTH
        if kind == 1:
            low, high = (low + 1, high) if up else (low, high - 1)
        first, stop = (low, middle) if part == 0 else (middle, high)
        if kind == 0:
            src_ref = C.at[pl.ds(first, stop - first), :, c_rows(c), :]
            dst_ref = C.at[pl.ds(first + shift, stop - first), :, c_rows(c), :]
        else:
            src_ref = K.at[pl.ds(first - 1, stop - first), core, k_rows(c), :]
            dst_ref = K.at[pl.ds(first - 1 + shift, stop - first), core, k_rows(c), :]
        sems = (way, 2 * kind + part, c)
        return remote(src_ref, dst_ref, z_send.at[sems], z_recv.at[sems], target, r)

    def z_start(c, owns):
        for q in range(2):
            part = q if owns else 1 - q

            @pl.when((p == q) & not_last)
            def _():
                for kind in (1, 0):
                    z_copy(c, kind, True, part).start()

            @pl.when((p == q) & not_first)
            def _():
                for kind in (1, 0):
                    z_copy(c, kind, False, part).start()

    def share(c, part, h):
        first, size = ((mates - 1, DEPTH), (0, STEPS - 1), (FIRST + 2 * DEPTH - 1, STEPS - 1))[part]
        ref = K.at[pl.ds(first, size), h, k_rows(c), :]
        return remote(ref, ref, sib_send.at[part, c], sib_recv.at[part, c], s, other_core)

    def pass_on(c):
        remote(
            SK.at[:, k_rows(c), :], K.at[pl.ds(mates - 1, DEPTH), core, k_rows(c), :],
            xk_send.at[c], xk_recv.at[c], mate, other_run,
        ).wait_recv()
        remote(
            SC.at[:, :, c_rows(c), :], C.at[pl.ds(mates, DEPTH), :, c_rows(c), :],
            xc_send.at[c], xc_recv.at[c], mate, r,
        ).wait_recv()

        if c > 0:
            z_start(c, True)
        z_start(c, False)
        share(c, 0, core).start()

    def pass_across(c):
        @pl.when(not_first)
        def _():
            for part in range(2):
                z_copy(c, 1, True, part).wait_recv()
            share(c, 1, core).start()

        @pl.when(not_last)
        def _():
            for part in range(2):
                z_copy(c, 1, False, part).wait_recv()
            share(c, 2, core).start()

    def halo_wait(c):
        share(c, 0, 1 - core).wait_recv()

        @pl.when(not_first)
        def _():
            for part in range(2):
                z_copy(c, 0, True, part).wait_recv()
            share(c, 1, 1 - core).wait_recv()

        @pl.when(not_last)
        def _():
            for part in range(2):
                z_copy(c, 0, False, part).wait_recv()
            share(c, 2, 1 - core).wait_recv()

    load_cot.wait()
    load_material.wait()
    fill_mates(0)
    fill_own(0)
    pl.semaphore_wait(
        barrier, 4 + (grid_z - 1) + (grid_y - 1) + not_first.astype(jnp.int32) + not_last.astype(jnp.int32)
    )
    for d in range(1, grid_y):
        y_rows(d, py).start()
    for copy in x_copies(0):
        copy.start()
    z_start(0, True)
    for c in range(1, len(in_chunks)):
        fill_mates(c)
        for copy in x_copies(c):
            copy.start()
        if c == 1:
            port_to_mate()
            pass_on(0)
        if c == min(2, len(in_chunks) - 1):
            port_along_z()
    for c in range(1, len(in_chunks)):
        fill_own(c)
        if PASS_AT[c] < 0:
            pass_on(c)

    lane = lax.broadcasted_iota(jnp.int32, (1, 1, 8, 128), 3)
    is_last, is_first = lane == 127, lane == 0

    def up_z(v):
        turned = pltpu.roll(v[0:1], 127, v.ndim - 1)
        turned = jnp.where(is_last if v.ndim == 4 else is_last[0], 0.0, turned)
        return jnp.concatenate([v[1:2], turned], 0)

    def down_z(v):
        turned = pltpu.roll(v[1:2], 1, v.ndim - 1)
        turned = jnp.where(is_first if v.ndim == 4 else is_first[0], 0.0, turned)
        return jnp.concatenate([turned, v[0:1]], 0)

    inside = not_first.astype(F32)

    def source_of(n, t, rows, ahead_rows, behind_rows):
        slot = window + t
        port_rows = gath.at[slot // (2 * grid_z), lax.rem(slot, 2 * grid_z)]
        drive = (0.5 * forcing_of(n - 1)) * port_rows[pl.ds(0, 2)]
        if n == 1:
            W[0, :, rows, :] = drive
            return drive, drive
        now = W[n - 2, :, rows, :]
        around = W[n - 2, :, ahead_rows, :] + W[n - 2, :, behind_rows, :] + up_z(now) + down_z(now)
        value = 2.0 * now + port_rows[pl.ds(2, 2)] * (around - 4.0 * now) + drive
        if n > 2:
            value = value - W[n - 3, :, rows, :]
        W[n - 1, :, rows, :] = value
        return value, value - now

    def add_driven(v, extra):
        return jnp.concatenate([v[:, 0:1] + extra[:, None], v[:, 1:2]], 1)

    def product(a):
        return a[:, 0] * a[:, 1]

    def first_step(t):
        rows = ds8(PAD + 8 * t, 8)
        ahead_rows, behind_rows = pl.ds(PAD + 8 * t + 1, 8), pl.ds(PAD + 8 * t - 1, 8)
        ie, ih = source_of(1, t, rows, ahead_rows, behind_rows)
        zero = jnp.zeros((2, 8, 128), F32)
        both = lambda d, e: jnp.stack([d, e], 1)
        follow = C[0, :, rows, :]
        gx_l = gy_l = gyd_l = None
        for i in range(LAYERS - 1):
            c = follow
            follow = C[i + 1, :, rows, :]
            gx = c - C[i, :, ahead_rows, :]
            gy = follow - c
            gyd = c - up_z(c)
            GX[i, :, :, rows, :] = both(zero, gx)
            GY[i, :, :, rows, :] = both(gyd, gy)
            GZ[i, :, :, rows, :] = both(-gx, zero)
            if i >= 1:
                if i == FIRST:
                    gx_l, gy_l, gyd_l = gx_l * inside, gy_l * inside, gyd_l * inside
                k = K[i - 1, :, rows, :]
                mask = K[i - 1, 0:1, pl.ds(0, 8), :]
                gx_y = gx - GX[i, :, 1, behind_rows, :]
                ex_d = c - k * (gx_y + (gyd - down_z(gyd)))
                ey_d = k * ((gx - gx_l) + mask * ih)
                ez_d = k * ((gyd - gyd_l) + mask * ie)
                ex_s = k * (down_z(gy) - gy)
                ey_s = k * (gx - down_z(gx))
                ez_s = c + k * ((gy - gy_l) - gx_y)
                EX[i - 1, :, :, rows, :] = both(ex_d, ex_s)
                EY[i - 1, :, :, rows, :] = both(ey_d, ey_s)
                EZ[i - 1, :, :, rows, :] = both(ez_d, ez_s)
                if FIRST <= i < FIRST + 2 * DEPTH:
                    GR[i - FIRST, :, rows, :] = ex_d * ex_s + ey_d * ey_s + ez_d * ez_s
            gx_l, gy_l, gyd_l = gx, gy, gyd

    def later_step(n, t):
        rows = ds8(PAD + 8 * t, 8)
        ahead_rows, behind_rows = pl.ds(PAD + 8 * t + 1, 8), pl.ds(PAD + 8 * t - 1, 8)
        ie, ih = source_of(n, t, rows, ahead_rows, behind_rows)
        ey_n, ez_n = EY[n - 2, :, :, rows, :], EZ[n - 2, :, :, rows, :]
        gy_l = gz_l = None
        for i in range(n - 1, LAYERS - n):
            ex, ey, ez = EX[i - 1, :, :, rows, :], ey_n, ez_n
            ey_n, ez_n = EY[i, :, :, rows, :], EZ[i, :, :, rows, :]
            gx = GX[i, :, :, rows, :] + ((ez - EZ[i - 1, :, :, ahead_rows, :]) + (up_z(ey) - ey))
            gy = GY[i, :, :, rows, :] + ((ex - up_z(ex)) + (ez_n - ez))
            gz = GZ[i, :, :, rows, :] + ((ey - ey_n) + (EX[i - 1, :, :, ahead_rows, :] - ex))
            GX[i, :, :, rows, :] = gx
            GY[i, :, :, rows, :] = gy
            GZ[i, :, :, rows, :] = gz
            if i >= n:
                if i == FIRST:
                    gy_l, gz_l = gy_l * inside, gz_l * inside
                k = K[i - 1, :, rows, :][:, None]
                mask = K[i - 1, 0:1, pl.ds(0, 8), :]
                ex = ex + k * ((gz - GZ[i, :, :, behind_rows, :]) - (gy - down_z(gy)))
                ey = ey + k * add_driven((gx - down_z(gx)) - (gz - gz_l), mask * ih)
                ez = ez + k * add_driven((gy - gy_l) - (gx - GX[i, :, :, behind_rows, :]), mask * ie)
                EX[i - 1, :, :, rows, :] = ex
                EY[i - 1, :, :, rows, :] = ey
                EZ[i - 1, :, :, rows, :] = ez
                if FIRST <= i < FIRST + 2 * DEPTH:
                    GR[i - FIRST, :, rows, :] = GR[i - FIRST, :, rows, :] + (product(ex) + product(ey) + product(ez))
            gy_l, gz_l = gy, gz

    def near_copy(j):
        first, stop = out_chunks[j]
        return remote(
            GR.at[:, 1 - core, ds8(PAD + 8 * (p + first), 8 * (stop - first)), :],
            near.at[:, pl.ds(8 * first, 8 * (stop - first)), :],
            near_send.at[j], near_recv.at[j], s, other_core,
        )

    def far_copies(j):
        first, stop = out_chunks[j]
        rows = pl.ds(8 * first, 8 * (stop - first))
        mine, theirs = pl.ds(DEPTH * p, DEPTH), pl.ds(DEPTH * (1 - p), DEPTH)
        return [
            remote(part.at[mine, rows, :], far.at[:, rows, :], far_send.at[0, j], far_recv.at[0, j], s, other_run),
            remote(part.at[theirs, rows, :], side.at[0, :, rows, :], far_send.at[1, j], far_recv.at[1, j], mate, r),
            remote(
                part.at[theirs, rows, :], side.at[1, :, rows, :], far_send.at[2, j], far_recv.at[2, j], mate, other_run
            ),
        ]

    def fin_copies(j):
        first, stop = out_chunks[j]
        copies = []
        for k in range(2):
            rows = ds8(half * k + 8 * first, 8 * (stop - first))
            src = fin.at[:, rows, :]
            dst = grad_h.at[:, core, rows, :]
            copies.append(
                (
                    pltpu.make_async_copy(src, dst, fin_copy.at[k, j]),
                    remote(src, dst, fin_send.at[k, j], fin_recv.at[k, j], s, other_core),
                    remote(
                        src, grad_h.at[:, 1 - core, rows, :],
                        fin_send.at[k, j], fin_recv.at[k, j], s, other_core,
                    ),
                )
            )
        return copies

    def field_copies(j):
        first, stop = out_chunks[j]
        size = 8 * (stop - first)
        src_rows = ds8(PAD + 8 * (p + first), size)
        dst = out_h.at[:, :, ds8(half * p + 8 * first, size), :]
        back = out_h.at[:, :, ds8(half * (1 - p) + 8 * first, size), :]
        src = EY.at[pl.ds(mates - 1, DEPTH), :, 0, src_rows, :]
        return [
            (
                pltpu.make_async_copy(EY.at[pl.ds(own - 1, DEPTH), :, 0, src_rows, :], dst, fo_copy.at[j]),
                remote(src, dst, fo_send.at[j], fo_recv.at[j], mate, r),
                remote(src, back, fo_send.at[j], fo_recv.at[j], mate, r),
            )
        ]

    def rows_done(j):
        near_copy(j).start()

    def sum_cores(j):
        first, stop = out_chunks[j]
        near_copy(j).wait_recv()

        def one(t, carry):
            rows = ds8(8 * t, 8)
            part[:, rows, :] = GR[:, core, ds8(PAD + 8 * (p + t), 8), :] + near[:, rows, :]
            return carry

        lax.fori_loop(first, stop, one, 0)
        for copy in far_copies(j):
            copy.start()
        for here, there, _ in field_copies(j):
            there.start()
            here.start()

    def sum_chips(j):
        first, stop = out_chunks[j]
        for copy in far_copies(j):
            copy.wait_recv()

        def one(t, carry):
            rows = ds8(8 * t, 8)
            fin[:, ds8(half * p + 8 * t, 8), :] = part[pl.ds(DEPTH * p, DEPTH), rows, :] + far[:, rows, :]
            fin[:, ds8(half * (1 - p) + 8 * t, 8), :] = side[0, :, rows, :] + side[1, :, rows, :]
            return carry

        lax.fori_loop(first, stop, one, 0)
        for here, there, _ in fin_copies(j):
            there.start()
            here.start()

    sweeps = tiles + STEPS - 1
    before, after, late = {}, {}, []
    for c in range(1, len(in_chunks)):
        at = in_chunks[c][0] - 1
        if PASS_AT[c] >= 0:
            before.setdefault(PASS_AT[c], []).append(functools.partial(pass_on, c))
        before.setdefault(max(0, at - 2), []).append(functools.partial(pass_across, c))
        before.setdefault(at, []).append(functools.partial(halo_wait, c))
    for j in range(len(out_chunks)):
        at = out_chunks[j][1] + STEPS - 1
        for event, delay in ((rows_done, 0), (sum_cores, 2), (sum_chips, 6)):
            if at + delay < sweeps:
                after.setdefault(at + delay, []).append(functools.partial(event, j))
            else:
                late.append((at + delay, functools.partial(event, j)))
    late.sort(key=lambda item: item[0])

    def at_sweep(T, table_of):
        for at, events in sorted(table_of.items()):

            @pl.when(T == at)
            def _():
                for event in events:
                    event()

    pass_across(0)
    port_wait()
    halo_wait(0)

    def sweep(T, carry):
        at_sweep(T, before)
        for n in range(1, STEPS + 1):
            t = T - (n - 1)
            high = tiles - 2 + p if n == STEPS else tiles - 1

            @pl.when((t >= 0) & (t <= high))
            def _():
                first_step(t) if n == 1 else later_step(n, t)

        at_sweep(T, after)
        return carry

    lax.fori_loop(0, sweeps, sweep, 0)
    for _, event in late:
        event()

    for j in range(len(out_chunks)):
        for here, there, back in fin_copies(j) + field_copies(j):
            here.wait()
            there.wait_send()
            back.wait_recv()
        near_copy(j).wait_send()
        for copy in far_copies(j):
            copy.wait_send()
    for d in range(1, grid_y):
        y_rows(d, py).wait_send()
    mate_rows(column).wait_send()
    for d in range(1, grid_z):
        z_rows(d, pz).wait_send()

    @pl.when(at_edge(pz))
    def _():
        for d in range(1, grid_z):
            edge_rows(d).wait_send()

    for c in range(len(in_chunks)):
        share(c, 0, core).wait_send()
        for copy in x_copies(c):
            copy.wait_send()

        @pl.when(not_last)
        def _():
            share(c, 2, core).wait_send()
            for kind in range(2):
                for part in range(2):
                    z_copy(c, kind, True, part).wait_send()

        @pl.when(not_first)
        def _():
            share(c, 1, core).wait_send()
            for kind in range(2):
                for part in range(2):
                    z_copy(c, kind, False, part).wait_send()


def local(slabs, grid_y, grid_z, material, eps_table, surface_mask, excite_map, mode_profiles, port_eps, cotangent):
    tiles = slabs // 2 + 1
    height = 8 * tiles + 2 * PAD
    half, rows = 4 * slabs, 8 * slabs
    chunks, outs = len(cuts(tiles, IN_SIZES)), len(cuts(tiles - 1, OUT_SIZES))
    vmem = lambda *shape: pltpu.VMEM(shape, F32)
    dma = lambda *shape: pltpu.SemaphoreType.DMA(shape)
    field = lambda layers: vmem(layers, 2, 2, height, 128)
    smem_spec = pl.BlockSpec(memory_space=pltpu.SMEM)
    vmem_spec = pl.BlockSpec(memory_space=pltpu.VMEM)
    any_spec = pl.BlockSpec(memory_space=pl.ANY)
    scratch = [
        vmem(LAYERS, 2, height, 128),
        vmem(LAYERS - 2, 2, height, 128),
        vmem(DEPTH, 2, height, 128),
        vmem(DEPTH, height, 128),
        pltpu.VMEM((DEPTH, rows, 256), jnp.int32),
        vmem(DEPTH, rows, 256),
        field(LAYERS - 2), field(LAYERS - 2), field(LAYERS - 2),
        field(LAYERS - 1), field(LAYERS - 1), field(LAYERS - 1),
        vmem(2 * DEPTH, 2, height, 128),
        vmem(STEPS, 2, height, 128),
        vmem(grid_y, 2 * grid_z, 4, 8, 128),
        vmem(2 * DEPTH, half, 128), vmem(2 * DEPTH, half, 128),
        vmem(DEPTH, half, 128), vmem(2, DEPTH, half, 128), vmem(DEPTH, rows, 128),
        dma(2), dma(grid_y + 2 * grid_z - 2), dma(grid_y + 2 * grid_z - 2),
        dma(chunks), dma(chunks), dma(chunks), dma(chunks), dma(2, 4, chunks), dma(2, 4, chunks),
        dma(3, chunks), dma(3, chunks),
        dma(outs), dma(outs), dma(3, outs), dma(3, outs),
        dma(2, outs), dma(2, outs), dma(2, outs), dma(outs), dma(outs), dma(outs),
    ]
    split = jax.ShapeDtypeStruct((DEPTH, 2, rows, 128), F32)
    grad_p, field_p = pl.pallas_call(
        functools.partial(kernel, slabs, grid_y, grid_z),
        out_shape=(split, split),
        in_specs=[smem_spec, smem_spec, smem_spec, vmem_spec, vmem_spec, any_spec, any_spec],
        out_specs=(any_spec, any_spec),
        scratch_shapes=scratch,
        compiler_params=pltpu.CompilerParams(
            collective_id=0, has_side_effects=True, vmem_limit_bytes=60 * 1024 * 1024
        ),
        cost_estimate=pl.CostEstimate(flops=600_000_000, bytes_accessed=6_000_000, transcendentals=0),
    )(eps_table, surface_mask, excite_map, mode_profiles, port_eps, material, cotangent)
    halves = pl.BlockSpec((1, 2, rows, 128), lambda x: (x, 0, 0, 0))
    return pl.pallas_call(
        restore,
        grid=(DEPTH,),
        out_shape=(
            jax.ShapeDtypeStruct(material.shape, F32),
            jax.ShapeDtypeStruct(cotangent.shape, F32),
        ),
        in_specs=[halves, halves],
        out_specs=(
            pl.BlockSpec((1, rows, 256), lambda x: (x, 0, 0)),
            pl.BlockSpec((1, 1, rows, 256), lambda x: (0, x, 0, 0)),
        ),
        compiler_params=pltpu.CompilerParams(vmem_limit_bytes=60 * 1024 * 1024),
    )(grad_p, field_p)


def solution(mesh):
    slabs = mesh.shape["slab"]
    grid_z = 4 if slabs == 32 else 2
    grid_y = slabs // 2 // grid_z
    in_specs = (
        P("slab", None, None),
        P(),
        P("slab"),
        P("run"),
        P(None, "slab", None),
        P("slab", None),
        P("run", "slab", None, None),
    )
    out_specs = (P("slab", None, None), P("run", "slab", None, None))
    return jax.shard_map(
        functools.partial(local, slabs, grid_y, grid_z),
        mesh=mesh, in_specs=in_specs, out_specs=out_specs, check_vma=False,
    )
```

```python
import functools
import math

import jax
import jax.numpy as jnp
from jax import lax
from jax.experimental import pallas as pl
from jax.experimental.pallas import tpu as pltpu
from jax.sharding import PartitionSpec as P

STEPS = 6
F32 = jnp.float32
DEPTH = 4
LAYERS = 2 * DEPTH + 2 * STEPS
PAD = 8
FIRST = STEPS
IN_SIZES = (2, 3, 4, 4, 4)
OUT_SIZES = (1, 2, 2, 2, 3, 3, 2, 1)
PASS_AT = (-1, -1, 0, 2, 5)


def forcing_of(n):
    t = float(n + 1)
    return 2.0 * math.sin(0.3 * t) * (1.0 - math.exp(-0.5 * t))


def cuts(total, sizes):
    spans, at = [], 0
    for size in sizes:
        if at < total:
            spans.append((at, min(total, at + size)))
            at += size
    if at < total:
        spans.append((at, total))
    return spans


def z_order(back):
    z = lax.broadcasted_iota(jnp.int32, (256, 256), 1 if back else 0)
    place = lax.broadcasted_iota(jnp.int32, (256, 256), 0 if back else 1)
    return (z == 2 * (place % 128) + place // 128).astype(F32).astype(jnp.bfloat16)


def reorder(v, order):
    high = v.astype(jnp.bfloat16)
    rest = v - high.astype(F32)
    middle = rest.astype(jnp.bfloat16)
    dot = lambda part: jnp.dot(part, order, preferred_element_type=F32)
    return dot(high) + dot(middle)


def restore(grad_p, field_p, grad, field):
    order = z_order(True)
    grad[0] = reorder(jnp.concatenate([grad_p[0, 0], grad_p[0, 1]], 1), order)
    field[0, 0] = reorder(jnp.concatenate([field_p[0, 0], field_p[0, 1]], 1), order)


def kernel(
    slabs, grid_y, grid_z,
    eps_s, mask_s, excite_s, profiles_v, port_v, material_h, cot_h,
    grad_h, out_h,
    C, K, SC, SK, MT, CR, EX, EY, EZ, GX, GY, GZ, GR, W, gath, near, part, far, side, fin,
    load_sem, port_send, port_recv, xc_send, xc_recv, xk_send, xk_recv, z_send, z_recv, sib_send, sib_recv,
    near_send, near_recv, far_send, far_recv, fin_copy, fin_send, fin_recv, fo_copy, fo_send, fo_recv,
):
    half = 4 * slabs
    tiles = slabs // 2 + 1
    rows_all = 8 * tiles
    pairs = slabs // 2
    in_chunks = cuts(tiles, IN_SIZES)
    out_chunks = cuts(tiles - 1, OUT_SIZES)
    s = lax.axis_index("slab")
    r = lax.axis_index("run")
    p = lax.rem(s, 2)
    m = s // 2
    core = lax.rem(r, 2)
    other_core = r + 1 - 2 * core
    other_run = lax.rem(r + 2, 4)
    mate = s + 1 - 2 * p
    py, pz = m // grid_z, lax.rem(m, grid_z)
    not_first, not_last = m > 0, m < pairs - 1
    window = p * (slabs // 2 - 1)
    base, mate_base = 8 * window, 8 * ((1 - p) * (slabs // 2 - 1))
    own, mates = FIRST + DEPTH * p, FIRST + DEPTH * (1 - p)

    def to(slab, run):
        return {"slab": slab, "run": run}

    def remote(src, dst, send, recv, slab, run):
        return pltpu.make_async_remote_copy(
            src_ref=src, dst_ref=dst, send_sem=send, recv_sem=recv,
            device_id=to(slab, run), device_id_type=pl.DeviceIdType.MESH,
        )

    def ds8(start, size):
        return pl.ds(pl.multiple_of(start, 8), size)

    load_cot = pltpu.make_async_copy(cot_h.at[0], CR, load_sem.at[0])
    load_material = pltpu.make_async_copy(material_h, MT, load_sem.at[1])
    load_cot.start()
    load_material.start()

    z_mates = [(py * grid_z + lax.rem(pz + d, grid_z)) * 2 + p for d in range(1, grid_z)]
    y_mates = [(lax.rem(py + d, grid_y) * grid_z + pz) * 2 + p for d in range(1, grid_y)]
    barrier = pltpu.get_barrier_semaphore()

    def hello(slab, run):
        pl.semaphore_signal(barrier, inc=1, device_id=to(slab, run), device_id_type=pl.DeviceIdType.MESH)

    hello(mate, r)
    hello(mate, other_run)
    hello(s, other_core)
    hello(s, other_run)

    for peer in z_mates + y_mates:
        hello(peer, r)

    @pl.when(not_first)
    def _():
        hello(s - 2, r)

    @pl.when(not_last)
    def _():
        hello(s + 2, r)

    picked = jnp.zeros((8, 256), F32)
    for j in range(4):
        picked = jnp.where(excite_s[0] == j, profiles_v[j], picked)
    port = 0.25 / port_v[...]
    order = z_order(False)
    port_block = reorder(jnp.concatenate([picked, port], 0), order)
    for h in range(2):
        gath[py, 2 * pz + p, h] = port_block[0:8, 128 * h : 128 * h + 128]
        gath[py, 2 * pz + p, 2 + h] = port_block[8:16, 128 * h : 128 * h + 128]

    zero_row = jnp.zeros((8, 128), F32)
    bottom = jnp.zeros((2, 2, 8, 128), F32)

    def clear(i, carry):
        C[i, :, pl.ds(PAD + rows_all, 8), :] = jnp.zeros((2, 8, 128), F32)
        return carry

    lax.fori_loop(0, LAYERS, clear, 0)

    def clear_fields(i, carry):
        EX[i, :, :, pl.ds(PAD + rows_all, 8), :] = bottom
        EZ[i, :, :, pl.ds(PAD + rows_all, 8), :] = bottom
        GX[i, :, :, pl.ds(0, 8), :] = bottom
        GZ[i, :, :, pl.ds(0, 8), :] = bottom
        return carry

    lax.fori_loop(0, LAYERS - 2, clear_fields, 0)
    GX[LAYERS - 2, :, :, pl.ds(0, 8), :] = bottom
    GZ[LAYERS - 2, :, :, pl.ds(0, 8), :] = bottom
    for n in range(STEPS):
        for edge in (0, PAD + rows_all):
            W[n, :, pl.ds(edge, 8), :] = jnp.zeros((2, 8, 128), F32)

    def clear_end(c_first, k_first):
        def one(t, carry):
            rows = ds8(8 * t, 8)
            C[pl.ds(c_first, STEPS), :, rows, :] = jnp.zeros((STEPS, 2, 8, 128), F32)
            K[pl.ds(k_first, STEPS - 1), :, rows, :] = jnp.zeros((STEPS - 1, 2, 8, 128), F32)
            return carry

        lax.fori_loop(0, tiles + 1, one, 0)

    @pl.when(m == 0)
    def _():
        clear_end(0, 0)

    @pl.when(m == pairs - 1)
    def _():
        clear_end(FIRST + 2 * DEPTH, FIRST + 2 * DEPTH - 1)

    def k_rows(c):
        start, stop = in_chunks[c]
        first = 0 if c == 0 else PAD + 8 * start
        return pl.ds(first, PAD + 8 * stop - first)

    def c_rows(c):
        start, stop = in_chunks[c]
        return pl.ds(PAD + 8 * start, 8 * (stop - start))

    for j in range(DEPTH):
        tile = jnp.full((8, 128), mask_s[j].astype(F32), F32)
        SK[j, pl.ds(0, 8), :] = tile
        for h in range(2):
            K[own - 1 + j, h, pl.ds(0, 8), :] = tile

    column = 2 * pz + p
    band = grid_y // 2

    def y_rows(d, y):
        rows = gath.at[y, column]
        return remote(rows, rows, port_send.at[d - 1], port_recv.at[d - 1], y_mates[d - 1], r)

    def mate_rows(place):
        rows = gath.at[:, place]
        return remote(rows, rows, port_send.at[grid_y - 1], port_recv.at[grid_y - 1], mate, r)

    def z_rows(d, z):
        rows = gath.at[pl.ds(band * p, band), pl.ds(2 * z, 2)]
        k = grid_y + d - 1
        return remote(rows, rows, port_send.at[k], port_recv.at[k], z_mates[d - 1], r)

    def edge_rows(d):
        rows = gath.at[band - p, (2 * grid_z - 1) * p]
        k = grid_y + grid_z + d - 2
        return remote(rows, rows, port_send.at[k], port_recv.at[k], z_mates[d - 1], r)

    def at_edge(z):
        return z == (grid_z - 1) * p

    def port_to_mate():
        for d in range(1, grid_y):
            y_rows(d, lax.rem(py - d + grid_y, grid_y)).wait_recv()
        mate_rows(column).start()

    def port_along_z():
        mate_rows(2 * pz + 1 - p).wait_recv()
        for d in range(1, grid_z):
            z_rows(d, pz).start()

        @pl.when(at_edge(pz))
        def _():
            for d in range(1, grid_z):
                edge_rows(d).start()

    def port_wait():
        for d in range(1, grid_z):
            source = lax.rem(pz - d + grid_z, grid_z)
            z_rows(d, source).wait_recv()

            @pl.when(at_edge(source))
            def _():
                edge_rows(d).wait_recv()

    def cot_rows(c, first):
        start, stop = in_chunks[c]
        size = 8 * (stop - start)
        v = CR[:, ds8(first + 8 * start, size), :].reshape(DEPTH * size, 256)
        return reorder(v, order).reshape(DEPTH, size, 256)

    table = [0.25 / jnp.full((1, 8, 128), eps_s[j], F32) for j in range(16)]

    def coefficient_of(index):
        rows = index.shape[1] // 8
        level = [jnp.concatenate([entry] * rows, 1) for entry in table]
        for bit in range(4):
            odd = ((index >> bit) & 1) != 0
            level = [jnp.where(odd, level[2 * j + 1], level[2 * j]) for j in range(len(level) // 2)]
        return level[0]

    def material_rows(c, first):
        start, stop = in_chunks[c]
        size = 8 * (stop - start)
        v = MT[:, ds8(first + 8 * start, size), :].reshape(DEPTH * size, 256).astype(F32).astype(jnp.bfloat16)
        return jnp.dot(v, order, preferred_element_type=F32).reshape(DEPTH, size, 256)

    def fill_mates(c):
        v = cot_rows(c, mate_base)
        for h in range(2):
            SC[:, h, c_rows(c), :] = v[:, :, 128 * h : 128 * h + 128]
        v = material_rows(c, mate_base)
        v = jnp.where(core == 0, v[:, :, :128], v[:, :, 128:])
        SK[:, c_rows(c), :] = coefficient_of(v.astype(jnp.int32))

    def fill_own(c):
        v = cot_rows(c, base)
        index = material_rows(c, base).astype(jnp.int32)
        for h in range(2):
            C[pl.ds(own, DEPTH), h, c_rows(c), :] = v[:, :, 128 * h : 128 * h + 128]
            K[pl.ds(own - 1, DEPTH), h, c_rows(c), :] = coefficient_of(index[:, :, 128 * h : 128 * h + 128])

    def x_copies(c):
        return [
            remote(
                SC.at[:, :, c_rows(c), :], C.at[pl.ds(own, DEPTH), :, c_rows(c), :], xc_send.at[c], xc_recv.at[c], mate, r
            ),
            remote(
                SK.at[:, k_rows(c), :], K.at[pl.ds(own - 1, DEPTH), core, k_rows(c), :],
                xk_send.at[c], xk_recv.at[c], mate, other_run,
            ),
        ]

    def z_copy(c, kind, up, part):
        way = 0 if up else 1
        target = s + 2 if up else s - 2
        middle = FIRST + DEPTH
        low, high = (FIRST + 2, FIRST + 2 * DEPTH) if up else (FIRST, FIRST + STEPS)
        shift = -2 * DEPTH if up else 2 * DEPTH
        if kind == 1:
            low, high = (low + 1, high) if up else (low, high - 1)
        first, stop = (low, middle) if part == 0 else (middle, high)
        if kind == 0:
            src_ref = C.at[pl.ds(first, stop - first), :, c_rows(c), :]
            dst_ref = C.at[pl.ds(first + shift, stop - first), :, c_rows(c), :]
        else:
            src_ref = K.at[pl.ds(first - 1, stop - first), core, k_rows(c), :]
            dst_ref = K.at[pl.ds(first - 1 + shift, stop - first), core, k_rows(c), :]
        sems = (way, 2 * kind + part, c)
        return remote(src_ref, dst_ref, z_send.at[sems], z_recv.at[sems], target, r)

    def z_start(c, owns):
        for q in range(2):
            part = q if owns else 1 - q

            @pl.when((p == q) & not_last)
            def _():
                for kind in (1, 0):
                    z_copy(c, kind, True, part).start()

            @pl.when((p == q) & not_first)
            def _():
                for kind in (1, 0):
                    z_copy(c, kind, False, part).start()

    def share(c, part, h):
        first, size = ((mates - 1, DEPTH), (0, STEPS - 1), (FIRST + 2 * DEPTH - 1, STEPS - 1))[part]
        ref = K.at[pl.ds(first, size), h, k_rows(c), :]
        return remote(ref, ref, sib_send.at[part, c], sib_recv.at[part, c], s, other_core)

    def pass_on(c):
        remote(
            SK.at[:, k_rows(c), :], K.at[pl.ds(mates - 1, DEPTH), core, k_rows(c), :],
            xk_send.at[c], xk_recv.at[c], mate, other_run,
        ).wait_recv()
        remote(
            SC.at[:, :, c_rows(c), :], C.at[pl.ds(mates, DEPTH), :, c_rows(c), :],
            xc_send.at[c], xc_recv.at[c], mate, r,
        ).wait_recv()

        if c > 0:
            z_start(c, True)
        z_start(c, False)
        share(c, 0, core).start()

    def pass_across(c):
        @pl.when(not_first)
        def _():
            for part in range(2):
                z_copy(c, 1, True, part).wait_recv()
            share(c, 1, core).start()

        @pl.when(not_last)
        def _():
            for part in range(2):
                z_copy(c, 1, False, part).wait_recv()
            share(c, 2, core).start()

    def halo_wait(c):
        share(c, 0, 1 - core).wait_recv()

        @pl.when(not_first)
        def _():
            for part in range(2):
                z_copy(c, 0, True, part).wait_recv()
            share(c, 1, 1 - core).wait_recv()

        @pl.when(not_last)
        def _():
            for part in range(2):
                z_copy(c, 0, False, part).wait_recv()
            share(c, 2, 1 - core).wait_recv()

    load_cot.wait()
    load_material.wait()
    fill_mates(0)
    fill_own(0)
    pl.semaphore_wait(
        barrier, 4 + (grid_z - 1) + (grid_y - 1) + not_first.astype(jnp.int32) + not_last.astype(jnp.int32)
    )
    for d in range(1, grid_y):
        y_rows(d, py).start()
    for copy in x_copies(0):
        copy.start()
    z_start(0, True)
    for c in range(1, len(in_chunks)):
        fill_mates(c)
        for copy in x_copies(c):
            copy.start()
        if c == 1:
            port_to_mate()
            pass_on(0)
        if c == min(2, len(in_chunks) - 1):
            port_along_z()
    for c in range(1, len(in_chunks)):
        fill_own(c)
        if PASS_AT[c] < 0:
            pass_on(c)

    lane = lax.broadcasted_iota(jnp.int32, (1, 1, 8, 128), 3)
    is_last, is_first = lane == 127, lane == 0

    def up_z(v):
        turned = pltpu.roll(v[0:1], 127, v.ndim - 1)
        turned = jnp.where(is_last if v.ndim == 4 else is_last[0], 0.0, turned)
        return jnp.concatenate([v[1:2], turned], 0)

    def down_z(v):
        turned = pltpu.roll(v[1:2], 1, v.ndim - 1)
        turned = jnp.where(is_first if v.ndim == 4 else is_first[0], 0.0, turned)
        return jnp.concatenate([turned, v[0:1]], 0)

    inside = not_first.astype(F32)

    def source_of(n, t, rows, ahead_rows, behind_rows):
        slot = window + t
        port_rows = gath.at[slot // (2 * grid_z), lax.rem(slot, 2 * grid_z)]
        drive = (0.5 * forcing_of(n - 1)) * port_rows[pl.ds(0, 2)]
        if n == 1:
            W[0, :, rows, :] = drive
            return drive, drive
        now = W[n - 2, :, rows, :]
        around = W[n - 2, :, ahead_rows, :] + W[n - 2, :, behind_rows, :] + up_z(now) + down_z(now)
        value = 2.0 * now + port_rows[pl.ds(2, 2)] * (around - 4.0 * now) + drive
        if n > 2:
            value = value - W[n - 3, :, rows, :]
        W[n - 1, :, rows, :] = value
        return value, value - now

    def add_driven(v, extra):
        return jnp.concatenate([v[:, 0:1] + extra[:, None], v[:, 1:2]], 1)

    def product(a):
        return a[:, 0] * a[:, 1]

    def first_step(t):
        rows = ds8(PAD + 8 * t, 8)
        ahead_rows, behind_rows = pl.ds(PAD + 8 * t + 1, 8), pl.ds(PAD + 8 * t - 1, 8)
        ie, ih = source_of(1, t, rows, ahead_rows, behind_rows)
        zero = jnp.zeros((2, 8, 128), F32)
        both = lambda d, e: jnp.stack([d, e], 1)
        follow = C[0, :, rows, :]
        gx_l = gy_l = gyd_l = None
        for i in range(LAYERS - 1):
            c = follow
            follow = C[i + 1, :, rows, :]
            gx = c - C[i, :, ahead_rows, :]
            gy = follow - c
            gyd = c - up_z(c)
            GX[i, :, :, rows, :] = both(zero, gx)
            GY[i, :, :, rows, :] = both(gyd, gy)
            GZ[i, :, :, rows, :] = both(-gx, zero)
            if i >= 1:
                if i == FIRST:
                    gx_l, gy_l, gyd_l = gx_l * inside, gy_l * inside, gyd_l * inside
                k = K[i - 1, :, rows, :]
                mask = K[i - 1, 0:1, pl.ds(0, 8), :]
                gx_y = gx - GX[i, :, 1, behind_rows, :]
                ex_d = c - k * (gx_y + (gyd - down_z(gyd)))
                ey_d = k * ((gx - gx_l) + mask * ih)
                ez_d = k * ((gyd - gyd_l) + mask * ie)
                ex_s = k * (down_z(gy) - gy)
                ey_s = k * (gx - down_z(gx))
                ez_s = c + k * ((gy - gy_l) - gx_y)
                EX[i - 1, :, :, rows, :] = both(ex_d, ex_s)
                EY[i - 1, :, :, rows, :] = both(ey_d, ey_s)
                EZ[i - 1, :, :, rows, :] = both(ez_d, ez_s)
                if FIRST <= i < FIRST + 2 * DEPTH:
                    GR[i - FIRST, :, rows, :] = ex_d * ex_s + ey_d * ey_s + ez_d * ez_s
            gx_l, gy_l, gyd_l = gx, gy, gyd

    def later_step(n, t):
        rows = ds8(PAD + 8 * t, 8)
        ahead_rows, behind_rows = pl.ds(PAD + 8 * t + 1, 8), pl.ds(PAD + 8 * t - 1, 8)
        ie, ih = source_of(n, t, rows, ahead_rows, behind_rows)
        ey_n, ez_n = EY[n - 2, :, :, rows, :], EZ[n - 2, :, :, rows, :]
        gy_l = gz_l = None
        for i in range(n - 1, LAYERS - n):
            ex, ey, ez = EX[i - 1, :, :, rows, :], ey_n, ez_n
            ey_n, ez_n = EY[i, :, :, rows, :], EZ[i, :, :, rows, :]
            gx = GX[i, :, :, rows, :] + ((ez - EZ[i - 1, :, :, ahead_rows, :]) + (up_z(ey) - ey))
            gy = GY[i, :, :, rows, :] + ((ex - up_z(ex)) + (ez_n - ez))
            gz = GZ[i, :, :, rows, :] + ((ey - ey_n) + (EX[i - 1, :, :, ahead_rows, :] - ex))
            GX[i, :, :, rows, :] = gx
            GY[i, :, :, rows, :] = gy
            GZ[i, :, :, rows, :] = gz
            if i >= n:
                if i == FIRST:
                    gy_l, gz_l = gy_l * inside, gz_l * inside
                k = K[i - 1, :, rows, :][:, None]
                mask = K[i - 1, 0:1, pl.ds(0, 8), :]
                ex = ex + k * ((gz - GZ[i, :, :, behind_rows, :]) - (gy - down_z(gy)))
                ey = ey + k * add_driven((gx - down_z(gx)) - (gz - gz_l), mask * ih)
                ez = ez + k * add_driven((gy - gy_l) - (gx - GX[i, :, :, behind_rows, :]), mask * ie)
                EX[i - 1, :, :, rows, :] = ex
                EY[i - 1, :, :, rows, :] = ey
                EZ[i - 1, :, :, rows, :] = ez
                if FIRST <= i < FIRST + 2 * DEPTH:
                    GR[i - FIRST, :, rows, :] = GR[i - FIRST, :, rows, :] + (product(ex) + product(ey) + product(ez))
            gy_l, gz_l = gy, gz

    def near_copy(j):
        first, stop = out_chunks[j]
        return remote(
            GR.at[:, 1 - core, ds8(PAD + 8 * (p + first), 8 * (stop - first)), :],
            near.at[:, pl.ds(8 * first, 8 * (stop - first)), :],
            near_send.at[j], near_recv.at[j], s, other_core,
        )

    def far_copies(j):
        first, stop = out_chunks[j]
        rows = pl.ds(8 * first, 8 * (stop - first))
        mine, theirs = pl.ds(DEPTH * p, DEPTH), pl.ds(DEPTH * (1 - p), DEPTH)
        return [
            remote(part.at[mine, rows, :], far.at[:, rows, :], far_send.at[0, j], far_recv.at[0, j], s, other_run),
            remote(part.at[theirs, rows, :], side.at[0, :, rows, :], far_send.at[1, j], far_recv.at[1, j], mate, r),
            remote(
                part.at[theirs, rows, :], side.at[1, :, rows, :], far_send.at[2, j], far_recv.at[2, j], mate, other_run
            ),
        ]

    def fin_copies(j):
        first, stop = out_chunks[j]
        copies = []
        for k in range(2):
            rows = ds8(half * k + 8 * first, 8 * (stop - first))
            src = fin.at[:, rows, :]
            dst = grad_h.at[:, core, rows, :]
            copies.append(
                (
                    pltpu.make_async_copy(src, dst, fin_copy.at[k, j]),
                    remote(src, dst, fin_send.at[k, j], fin_recv.at[k, j], s, other_core),
                    remote(
                        src, grad_h.at[:, 1 - core, rows, :],
                        fin_send.at[k, j], fin_recv.at[k, j], s, other_core,
                    ),
                )
            )
        return copies

    def field_copies(j):
        first, stop = out_chunks[j]
        size = 8 * (stop - first)
        src_rows = ds8(PAD + 8 * (p + first), size)
        dst = out_h.at[:, :, ds8(half * p + 8 * first, size), :]
        back = out_h.at[:, :, ds8(half * (1 - p) + 8 * first, size), :]
        src = EY.at[pl.ds(mates - 1, DEPTH), :, 0, src_rows, :]
        return [
            (
                pltpu.make_async_copy(EY.at[pl.ds(own - 1, DEPTH), :, 0, src_rows, :], dst, fo_copy.at[j]),
                remote(src, dst, fo_send.at[j], fo_recv.at[j], mate, r),
                remote(src, back, fo_send.at[j], fo_recv.at[j], mate, r),
            )
        ]

    def fields_start(j):
        for here, there, _ in field_copies(j):
            there.start()
            here.start()

    def rows_done(j):
        near_copy(j).start()
        if j < len(out_chunks) - 2:
            fields_start(j)

    def sum_cores(j):
        first, stop = out_chunks[j]
        near_copy(j).wait_recv()

        def one(t, carry):
            rows = ds8(8 * t, 8)
            part[:, rows, :] = GR[:, core, ds8(PAD + 8 * (p + t), 8), :] + near[:, rows, :]
            return carry

        lax.fori_loop(first, stop, one, 0)
        for copy in far_copies(j):
            copy.start()
        if j >= len(out_chunks) - 2:
            fields_start(j)

    def sum_chips(j):
        first, stop = out_chunks[j]
        for copy in far_copies(j):
            copy.wait_recv()

        def one(t, carry):
            rows = ds8(8 * t, 8)
            fin[:, ds8(half * p + 8 * t, 8), :] = part[pl.ds(DEPTH * p, DEPTH), rows, :] + far[:, rows, :]
            fin[:, ds8(half * (1 - p) + 8 * t, 8), :] = side[0, :, rows, :] + side[1, :, rows, :]
            return carry

        lax.fori_loop(first, stop, one, 0)
        for here, there, _ in fin_copies(j):
            there.start()
            here.start()

    sweeps = tiles + STEPS - 1
    before, after, late = {}, {}, []
    for c in range(1, len(in_chunks)):
        at = in_chunks[c][0] - 1
        if PASS_AT[c] >= 0:
            before.setdefault(PASS_AT[c], []).append(functools.partial(pass_on, c))
        before.setdefault(max(0, at - 2), []).append(functools.partial(pass_across, c))
        before.setdefault(at, []).append(functools.partial(halo_wait, c))
    for j in range(len(out_chunks)):
        at = out_chunks[j][1] + STEPS - 1
        for event, delay in ((rows_done, 0), (sum_cores, 1), (sum_chips, 5)):
            if at + delay < sweeps:
                after.setdefault(at + delay, []).append(functools.partial(event, j))
            else:
                late.append((at + delay, functools.partial(event, j)))
    late.sort(key=lambda item: item[0])

    def at_sweep(T, table_of):
        for at, events in sorted(table_of.items()):

            @pl.when(T == at)
            def _():
                for event in events:
                    event()

    pass_across(0)
    port_wait()
    halo_wait(0)

    def sweep(T, carry):
        at_sweep(T, before)
        for n in range(1, STEPS + 1):
            t = T - (n - 1)
            high = tiles - 2 + p if n == STEPS else tiles - 1

            @pl.when((t >= 0) & (t <= high))
            def _():
                first_step(t) if n == 1 else later_step(n, t)

        at_sweep(T, after)
        return carry

    lax.fori_loop(0, sweeps, sweep, 0)
    for _, event in late:
        event()

    for j in range(len(out_chunks)):
        for here, there, back in fin_copies(j) + field_copies(j):
            here.wait()
            there.wait_send()
            back.wait_recv()
        near_copy(j).wait_send()
        for copy in far_copies(j):
            copy.wait_send()
    for d in range(1, grid_y):
        y_rows(d, py).wait_send()
    mate_rows(column).wait_send()
    for d in range(1, grid_z):
        z_rows(d, pz).wait_send()

    @pl.when(at_edge(pz))
    def _():
        for d in range(1, grid_z):
            edge_rows(d).wait_send()

    for c in range(len(in_chunks)):
        share(c, 0, core).wait_send()
        for copy in x_copies(c):
            copy.wait_send()

        @pl.when(not_last)
        def _():
            share(c, 2, core).wait_send()
            for kind in range(2):
                for part in range(2):
                    z_copy(c, kind, True, part).wait_send()

        @pl.when(not_first)
        def _():
            share(c, 1, core).wait_send()
            for kind in range(2):
                for part in range(2):
                    z_copy(c, kind, False, part).wait_send()


def local(slabs, grid_y, grid_z, material, eps_table, surface_mask, excite_map, mode_profiles, port_eps, cotangent):
    tiles = slabs // 2 + 1
    height = 8 * tiles + 2 * PAD
    half, rows = 4 * slabs, 8 * slabs
    chunks, outs = len(cuts(tiles, IN_SIZES)), len(cuts(tiles - 1, OUT_SIZES))
    vmem = lambda *shape: pltpu.VMEM(shape, F32)
    dma = lambda *shape: pltpu.SemaphoreType.DMA(shape)
    field = lambda layers: vmem(layers, 2, 2, height, 128)
    smem_spec = pl.BlockSpec(memory_space=pltpu.SMEM)
    vmem_spec = pl.BlockSpec(memory_space=pltpu.VMEM)
    any_spec = pl.BlockSpec(memory_space=pl.ANY)
    scratch = [
        vmem(LAYERS, 2, height, 128),
        vmem(LAYERS - 2, 2, height, 128),
        vmem(DEPTH, 2, height, 128),
        vmem(DEPTH, height, 128),
        pltpu.VMEM((DEPTH, rows, 256), jnp.int32),
        vmem(DEPTH, rows, 256),
        field(LAYERS - 2), field(LAYERS - 2), field(LAYERS - 2),
        field(LAYERS - 1), field(LAYERS - 1), field(LAYERS - 1),
        vmem(2 * DEPTH, 2, height, 128),
        vmem(STEPS, 2, height, 128),
        vmem(grid_y, 2 * grid_z, 4, 8, 128),
        vmem(2 * DEPTH, half, 128), vmem(2 * DEPTH, half, 128),
        vmem(DEPTH, half, 128), vmem(2, DEPTH, half, 128), vmem(DEPTH, rows, 128),
        dma(2), dma(grid_y + 2 * grid_z - 2), dma(grid_y + 2 * grid_z - 2),
        dma(chunks), dma(chunks), dma(chunks), dma(chunks), dma(2, 4, chunks), dma(2, 4, chunks),
        dma(3, chunks), dma(3, chunks),
        dma(outs), dma(outs), dma(3, outs), dma(3, outs),
        dma(2, outs), dma(2, outs), dma(2, outs), dma(outs), dma(outs), dma(outs),
    ]
    split = jax.ShapeDtypeStruct((DEPTH, 2, rows, 128), F32)
    grad_p, field_p = pl.pallas_call(
        functools.partial(kernel, slabs, grid_y, grid_z),
        out_shape=(split, split),
        in_specs=[smem_spec, smem_spec, smem_spec, vmem_spec, vmem_spec, any_spec, any_spec],
        out_specs=(any_spec, any_spec),
        scratch_shapes=scratch,
        compiler_params=pltpu.CompilerParams(
            collective_id=0, has_side_effects=True, vmem_limit_bytes=60 * 1024 * 1024
        ),
        cost_estimate=pl.CostEstimate(flops=600_000_000, bytes_accessed=6_000_000, transcendentals=0),
    )(eps_table, surface_mask, excite_map, mode_profiles, port_eps, material, cotangent)
    halves = pl.BlockSpec((1, 2, rows, 128), lambda x: (x, 0, 0, 0))
    return pl.pallas_call(
        restore,
        grid=(DEPTH,),
        out_shape=(
            jax.ShapeDtypeStruct(material.shape, F32),
            jax.ShapeDtypeStruct(cotangent.shape, F32),
        ),
        in_specs=[halves, halves],
        out_specs=(
            pl.BlockSpec((1, rows, 256), lambda x: (x, 0, 0)),
            pl.BlockSpec((1, 1, rows, 256), lambda x: (0, x, 0, 0)),
        ),
        compiler_params=pltpu.CompilerParams(vmem_limit_bytes=60 * 1024 * 1024),
    )(grad_p, field_p)


def solution(mesh):
    slabs = mesh.shape["slab"]
    grid_z = 4 if slabs == 32 else 2
    grid_y = slabs // 2 // grid_z
    in_specs = (
        P("slab", None, None),
        P(),
        P("slab"),
        P("run"),
        P(None, "slab", None),
        P("slab", None),
        P("run", "slab", None, None),
    )
    out_specs = (P("slab", None, None), P("run", "slab", None, None))
    return jax.shard_map(
        functools.partial(local, slabs, grid_y, grid_z),
        mesh=mesh, in_specs=in_specs, out_specs=out_specs, check_vma=False,
    )
```

```python
import functools
import math

import jax
import jax.numpy as jnp
from jax import lax
from jax.experimental import pallas as pl
from jax.experimental.pallas import tpu as pltpu
from jax.sharding import PartitionSpec as P

STEPS = 6
F32 = jnp.float32
DEPTH = 4
LAYERS = 2 * DEPTH + 2 * STEPS
PAD = 8
FIRST = STEPS
IN_SIZES = (2, 3, 4, 4, 4)
OUT_SIZES = (1, 2, 2, 2, 3, 3, 2, 1)
PASS_AT = (-1, -1, 0, 2, 5)


def forcing_of(n):
    t = float(n + 1)
    return 2.0 * math.sin(0.3 * t) * (1.0 - math.exp(-0.5 * t))


def cuts(total, sizes):
    spans, at = [], 0
    for size in sizes:
        if at < total:
            spans.append((at, min(total, at + size)))
            at += size
    if at < total:
        spans.append((at, total))
    return spans


def z_order(back):
    z = lax.broadcasted_iota(jnp.int32, (256, 256), 1 if back else 0)
    place = lax.broadcasted_iota(jnp.int32, (256, 256), 0 if back else 1)
    return (z == 2 * (place % 128) + place // 128).astype(F32).astype(jnp.bfloat16)


def reorder(v, order):
    high = v.astype(jnp.bfloat16)
    rest = v - high.astype(F32)
    middle = rest.astype(jnp.bfloat16)
    dot = lambda part: jnp.dot(part, order, preferred_element_type=F32)
    return dot(high) + dot(middle)


def restore(grad_p, field_p, grad, field):
    order = z_order(True)
    grad[0] = reorder(jnp.concatenate([grad_p[0, 0], grad_p[0, 1]], 1), order)
    field[0, 0] = reorder(jnp.concatenate([field_p[0, 0], field_p[0, 1]], 1), order)


def kernel(
    slabs, grid_y, grid_z,
    eps_s, mask_s, excite_s, profiles_v, port_v, material_h, cot_h,
    grad_h, out_h,
    C, K, SC, SK, MT, CR, EX, EY, EZ, GX, GY, GZ, GR, W, gath, near, part, far, side, fin,
    load_sem, port_send, port_recv, xc_send, xc_recv, xk_send, xk_recv, z_send, z_recv, sib_send, sib_recv,
    near_send, near_recv, far_send, far_recv, fin_copy, fin_send, fin_recv, fo_copy, fo_send, fo_recv,
):
    half = 4 * slabs
    tiles = slabs // 2 + 1
    rows_all = 8 * tiles
    pairs = slabs // 2
    in_chunks = cuts(tiles, IN_SIZES)
    out_chunks = cuts(tiles - 1, OUT_SIZES)
    s = lax.axis_index("slab")
    r = lax.axis_index("run")
    p = lax.rem(s, 2)
    m = s // 2
    core = lax.rem(r, 2)
    other_core = r + 1 - 2 * core
    other_run = lax.rem(r + 2, 4)
    mate = s + 1 - 2 * p
    py, pz = m // grid_z, lax.rem(m, grid_z)
    not_first, not_last = m > 0, m < pairs - 1
    window = p * (slabs // 2 - 1)
    base, mate_base = 8 * window, 8 * ((1 - p) * (slabs // 2 - 1))
    own, mates = FIRST + DEPTH * p, FIRST + DEPTH * (1 - p)

    def to(slab, run):
        return {"slab": slab, "run": run}

    def remote(src, dst, send, recv, slab, run):
        return pltpu.make_async_remote_copy(
            src_ref=src, dst_ref=dst, send_sem=send, recv_sem=recv,
            device_id=to(slab, run), device_id_type=pl.DeviceIdType.MESH,
        )

    def ds8(start, size):
        return pl.ds(pl.multiple_of(start, 8), size)

    load_cot = pltpu.make_async_copy(cot_h.at[0], CR, load_sem.at[0])
    load_material = pltpu.make_async_copy(material_h, MT, load_sem.at[1])
    load_cot.start()
    load_material.start()

    z_mates = [(py * grid_z + lax.rem(pz + d, grid_z)) * 2 + p for d in range(1, grid_z)]
    y_mates = [(lax.rem(py + d, grid_y) * grid_z + pz) * 2 + p for d in range(1, grid_y)]
    barrier = pltpu.get_barrier_semaphore()

    def hello(slab, run):
        pl.semaphore_signal(barrier, inc=1, device_id=to(slab, run), device_id_type=pl.DeviceIdType.MESH)

    hello(mate, r)
    hello(mate, other_run)
    hello(s, other_core)
    hello(s, other_run)

    for peer in z_mates + y_mates:
        hello(peer, r)

    @pl.when(not_first)
    def _():
        hello(s - 2, r)

    @pl.when(not_last)
    def _():
        hello(s + 2, r)

    picked = jnp.zeros((8, 256), F32)
    for j in range(4):
        picked = jnp.where(excite_s[0] == j, profiles_v[j], picked)
    port = 0.25 / port_v[...]
    order = z_order(False)
    port_block = reorder(jnp.concatenate([picked, port], 0), order)
    for h in range(2):
        gath[py, 2 * pz + p, h] = port_block[0:8, 128 * h : 128 * h + 128]
        gath[py, 2 * pz + p, 2 + h] = port_block[8:16, 128 * h : 128 * h + 128]

    zero_row = jnp.zeros((8, 128), F32)
    bottom = jnp.zeros((2, 2, 8, 128), F32)

    def clear(i, carry):
        C[i, :, pl.ds(PAD + rows_all, 8), :] = jnp.zeros((2, 8, 128), F32)
        return carry

    lax.fori_loop(0, LAYERS, clear, 0)

    def clear_fields(i, carry):
        EX[i, :, :, pl.ds(PAD + rows_all, 8), :] = bottom
        EZ[i, :, :, pl.ds(PAD + rows_all, 8), :] = bottom
        GX[i, :, :, pl.ds(0, 8), :] = bottom
        GZ[i, :, :, pl.ds(0, 8), :] = bottom
        return carry

    lax.fori_loop(0, LAYERS - 2, clear_fields, 0)
    GX[LAYERS - 2, :, :, pl.ds(0, 8), :] = bottom
    GZ[LAYERS - 2, :, :, pl.ds(0, 8), :] = bottom
    for n in range(STEPS):
        for edge in (0, PAD + rows_all):
            W[n, :, pl.ds(edge, 8), :] = jnp.zeros((2, 8, 128), F32)

    def clear_end(c_first, k_first):
        def one(t, carry):
            rows = ds8(8 * t, 8)
            C[pl.ds(c_first, STEPS), :, rows, :] = jnp.zeros((STEPS, 2, 8, 128), F32)
            K[pl.ds(k_first, STEPS - 1), :, rows, :] = jnp.zeros((STEPS - 1, 2, 8, 128), F32)
            return carry

        lax.fori_loop(0, tiles + 1, one, 0)

    @pl.when(m == 0)
    def _():
        clear_end(0, 0)

    @pl.when(m == pairs - 1)
    def _():
        clear_end(FIRST + 2 * DEPTH, FIRST + 2 * DEPTH - 1)

    def k_rows(c):
        start, stop = in_chunks[c]
        first = 0 if c == 0 else PAD + 8 * start
        return pl.ds(first, PAD + 8 * stop - first)

    def c_rows(c):
        start, stop = in_chunks[c]
        return pl.ds(PAD + 8 * start, 8 * (stop - start))

    for j in range(DEPTH):
        tile = jnp.full((8, 128), mask_s[j].astype(F32), F32)
        SK[j, pl.ds(0, 8), :] = tile
        for h in range(2):
            K[own - 1 + j, h, pl.ds(0, 8), :] = tile

    column = 2 * pz + p
    band = grid_y // 2

    def y_rows(d, y):
        rows = gath.at[y, column]
        return remote(rows, rows, port_send.at[d - 1], port_recv.at[d - 1], y_mates[d - 1], r)

    def mate_rows(place):
        rows = gath.at[:, place]
        return remote(rows, rows, port_send.at[grid_y - 1], port_recv.at[grid_y - 1], mate, r)

    def z_rows(d, z):
        rows = gath.at[pl.ds(band * p, band), pl.ds(2 * z, 2)]
        k = grid_y + d - 1
        return remote(rows, rows, port_send.at[k], port_recv.at[k], z_mates[d - 1], r)

    def edge_rows(d):
        rows = gath.at[band - p, (2 * grid_z - 1) * p]
        k = grid_y + grid_z + d - 2
        return remote(rows, rows, port_send.at[k], port_recv.at[k], z_mates[d - 1], r)

    def at_edge(z):
        return z == (grid_z - 1) * p

    def port_to_mate():
        for d in range(1, grid_y):
            y_rows(d, lax.rem(py - d + grid_y, grid_y)).wait_recv()
        mate_rows(column).start()

    def port_along_z():
        mate_rows(2 * pz + 1 - p).wait_recv()
        for d in range(1, grid_z):
            z_rows(d, pz).start()

        @pl.when(at_edge(pz))
        def _():
            for d in range(1, grid_z):
                edge_rows(d).start()

    def port_wait():
        for d in range(1, grid_z):
            source = lax.rem(pz - d + grid_z, grid_z)
            z_rows(d, source).wait_recv()

            @pl.when(at_edge(source))
            def _():
                edge_rows(d).wait_recv()

    def cot_rows(c, first):
        start, stop = in_chunks[c]
        size = 8 * (stop - start)
        v = CR[:, ds8(first + 8 * start, size), :].reshape(DEPTH * size, 256)
        return reorder(v, order).reshape(DEPTH, size, 256)

    table = [0.25 / jnp.full((1, 8, 128), eps_s[j], F32) for j in range(16)]

    def coefficient_of(index):
        rows = index.shape[1] // 8
        level = [jnp.concatenate([entry] * rows, 1) for entry in table]
        for bit in range(4):
            odd = ((index >> bit) & 1) != 0
            level = [jnp.where(odd, level[2 * j + 1], level[2 * j]) for j in range(len(level) // 2)]
        return level[0]

    def material_rows(c, first):
        start, stop = in_chunks[c]
        size = 8 * (stop - start)
        v = MT[:, ds8(first + 8 * start, size), :].reshape(DEPTH * size, 256).astype(F32).astype(jnp.bfloat16)
        return jnp.dot(v, order, preferred_element_type=F32).reshape(DEPTH, size, 256)

    def fill_mates(c):
        v = cot_rows(c, mate_base)
        for h in range(2):
            SC[:, h, c_rows(c), :] = v[:, :, 128 * h : 128 * h + 128]
        v = material_rows(c, mate_base)
        v = jnp.where(core == 0, v[:, :, :128], v[:, :, 128:])
        SK[:, c_rows(c), :] = coefficient_of(v.astype(jnp.int32))

    def fill_own(c):
        v = cot_rows(c, base)
        index = material_rows(c, base).astype(jnp.int32)
        for h in range(2):
            C[pl.ds(own, DEPTH), h, c_rows(c), :] = v[:, :, 128 * h : 128 * h + 128]
            K[pl.ds(own - 1, DEPTH), h, c_rows(c), :] = coefficient_of(index[:, :, 128 * h : 128 * h + 128])

    def x_copies(c):
        return [
            remote(
                SC.at[:, :, c_rows(c), :], C.at[pl.ds(own, DEPTH), :, c_rows(c), :], xc_send.at[c], xc_recv.at[c], mate, r
            ),
            remote(
                SK.at[:, k_rows(c), :], K.at[pl.ds(own - 1, DEPTH), core, k_rows(c), :],
                xk_send.at[c], xk_recv.at[c], mate, other_run,
            ),
        ]

    def z_copy(c, kind, up, part):
        way = 0 if up else 1
        target = s + 2 if up else s - 2
        middle = FIRST + DEPTH
        low, high = (FIRST + 2, FIRST + 2 * DEPTH) if up else (FIRST, FIRST + STEPS)
        shift = -2 * DEPTH if up else 2 * DEPTH
        if kind == 1:
            low, high = (low + 1, high) if up else (low, high - 1)
        first, stop = (low, middle) if part == 0 else (middle, high)
        if kind == 0:
            src_ref = C.at[pl.ds(first, stop - first), :, c_rows(c), :]
            dst_ref = C.at[pl.ds(first + shift, stop - first), :, c_rows(c), :]
        else:
            src_ref = K.at[pl.ds(first - 1, stop - first), core, k_rows(c), :]
            dst_ref = K.at[pl.ds(first - 1 + shift, stop - first), core, k_rows(c), :]
        sems = (way, 2 * kind + part, c)
        return remote(src_ref, dst_ref, z_send.at[sems], z_recv.at[sems], target, r)

    def z_start(c, owns):
        for q in range(2):
            part = q if owns else 1 - q

            @pl.when((p == q) & not_last)
            def _():
                for kind in (1, 0):
                    z_copy(c, kind, True, part).start()

            @pl.when((p == q) & not_first)
            def _():
                for kind in (1, 0):
                    z_copy(c, kind, False, part).start()

    def share(c, part, h):
        first, size = ((mates - 1, DEPTH), (0, STEPS - 1), (FIRST + 2 * DEPTH - 1, STEPS - 1))[part]
        ref = K.at[pl.ds(first, size), h, k_rows(c), :]
        return remote(ref, ref, sib_send.at[part, c], sib_recv.at[part, c], s, other_core)

    def pass_on(c):
        remote(
            SK.at[:, k_rows(c), :], K.at[pl.ds(mates - 1, DEPTH), core, k_rows(c), :],
            xk_send.at[c], xk_recv.at[c], mate, other_run,
        ).wait_recv()
        remote(
            SC.at[:, :, c_rows(c), :], C.at[pl.ds(mates, DEPTH), :, c_rows(c), :],
            xc_send.at[c], xc_recv.at[c], mate, r,
        ).wait_recv()

        if c > 0:
            z_start(c, True)
        z_start(c, False)
        share(c, 0, core).start()

    def pass_across(c):
        @pl.when(not_first)
        def _():
            for part in range(2):
                z_copy(c, 1, True, part).wait_recv()
            share(c, 1, core).start()

        @pl.when(not_last)
        def _():
            for part in range(2):
                z_copy(c, 1, False, part).wait_recv()
            share(c, 2, core).start()

    def halo_wait(c):
        share(c, 0, 1 - core).wait_recv()

        @pl.when(not_first)
        def _():
            for part in range(2):
                z_copy(c, 0, True, part).wait_recv()
            share(c, 1, 1 - core).wait_recv()

        @pl.when(not_last)
        def _():
            for part in range(2):
                z_copy(c, 0, False, part).wait_recv()
            share(c, 2, 1 - core).wait_recv()

    load_cot.wait()
    load_material.wait()
    fill_mates(0)
    fill_own(0)
    pl.semaphore_wait(
        barrier, 4 + (grid_z - 1) + (grid_y - 1) + not_first.astype(jnp.int32) + not_last.astype(jnp.int32)
    )
    for d in range(1, grid_y):
        y_rows(d, py).start()
    for copy in x_copies(0):
        copy.start()
    z_start(0, True)
    for c in range(1, len(in_chunks)):
        fill_mates(c)
        for copy in x_copies(c):
            copy.start()
        if c == 1:
            port_to_mate()
            pass_on(0)
        if c == min(2, len(in_chunks) - 1):
            port_along_z()
    for c in range(1, len(in_chunks)):
        fill_own(c)
        if PASS_AT[c] < 0:
            pass_on(c)

    lane = lax.broadcasted_iota(jnp.int32, (1, 1, 8, 128), 3)
    is_last, is_first = lane == 127, lane == 0

    def up_z(v):
        turned = pltpu.roll(v[0:1], 127, v.ndim - 1)
        turned = jnp.where(is_last if v.ndim == 4 else is_last[0], 0.0, turned)
        return jnp.concatenate([v[1:2], turned], 0)

    def down_z(v):
        turned = pltpu.roll(v[1:2], 1, v.ndim - 1)
        turned = jnp.where(is_first if v.ndim == 4 else is_first[0], 0.0, turned)
        return jnp.concatenate([turned, v[0:1]], 0)

    inside = not_first.astype(F32)

    def source_of(n, t, rows, ahead_rows, behind_rows):
        slot = window + t
        port_rows = gath.at[slot // (2 * grid_z), lax.rem(slot, 2 * grid_z)]
        drive = (0.5 * forcing_of(n - 1)) * port_rows[pl.ds(0, 2)]
        if n == 1:
            W[0, :, rows, :] = drive
            return drive, drive
        now = W[n - 2, :, rows, :]
        around = W[n - 2, :, ahead_rows, :] + W[n - 2, :, behind_rows, :] + up_z(now) + down_z(now)
        value = 2.0 * now + port_rows[pl.ds(2, 2)] * (around - 4.0 * now) + drive
        if n > 2:
            value = value - W[n - 3, :, rows, :]
        W[n - 1, :, rows, :] = value
        return value, value - now

    def add_driven(v, extra):
        return jnp.concatenate([v[:, 0:1] + extra[:, None], v[:, 1:2]], 1)

    def product(a):
        return a[:, 0] * a[:, 1]

    def first_step(t):
        rows = ds8(PAD + 8 * t, 8)
        ahead_rows, behind_rows = pl.ds(PAD + 8 * t + 1, 8), pl.ds(PAD + 8 * t - 1, 8)
        ie, ih = source_of(1, t, rows, ahead_rows, behind_rows)
        zero = jnp.zeros((2, 8, 128), F32)
        both = lambda d, e: jnp.stack([d, e], 1)
        follow = C[0, :, rows, :]
        gx_l = gy_l = gyd_l = None
        for i in range(LAYERS - 1):
            c = follow
            follow = C[i + 1, :, rows, :]
            gx = c - C[i, :, ahead_rows, :]
            gy = follow - c
            gyd = c - up_z(c)
            GX[i, :, :, rows, :] = both(zero, gx)
            GY[i, :, :, rows, :] = both(gyd, gy)
            GZ[i, :, :, rows, :] = both(-gx, zero)
            if i >= 1:
                if i == FIRST:
                    gx_l, gy_l, gyd_l = gx_l * inside, gy_l * inside, gyd_l * inside
                k = K[i - 1, :, rows, :]
                mask = K[i - 1, 0:1, pl.ds(0, 8), :]
                gx_y = gx - GX[i, :, 1, behind_rows, :]
                ex_d = c - k * (gx_y + (gyd - down_z(gyd)))
                ey_d = k * ((gx - gx_l) + mask * ih)
                ez_d = k * ((gyd - gyd_l) + mask * ie)
                ex_s = k * (down_z(gy) - gy)
                ey_s = k * (gx - down_z(gx))
                ez_s = c + k * ((gy - gy_l) - gx_y)
                EX[i - 1, :, :, rows, :] = both(ex_d, ex_s)
                EY[i - 1, :, :, rows, :] = both(ey_d, ey_s)
                EZ[i - 1, :, :, rows, :] = both(ez_d, ez_s)
                if FIRST <= i < FIRST + 2 * DEPTH:
                    GR[i - FIRST, :, rows, :] = ex_d * ex_s + ey_d * ey_s + ez_d * ez_s
            gx_l, gy_l, gyd_l = gx, gy, gyd

    def later_step(n, t):
        rows = ds8(PAD + 8 * t, 8)
        ahead_rows, behind_rows = pl.ds(PAD + 8 * t + 1, 8), pl.ds(PAD + 8 * t - 1, 8)
        ie, ih = source_of(n, t, rows, ahead_rows, behind_rows)
        ey_n, ez_n = EY[n - 2, :, :, rows, :], EZ[n - 2, :, :, rows, :]
        gy_l = gz_l = None
        for i in range(n - 1, LAYERS - n):
            ex, ey, ez = EX[i - 1, :, :, rows, :], ey_n, ez_n
            ey_n, ez_n = EY[i, :, :, rows, :], EZ[i, :, :, rows, :]
            gx = GX[i, :, :, rows, :] + ((ez - EZ[i - 1, :, :, ahead_rows, :]) + (up_z(ey) - ey))
            gy = GY[i, :, :, rows, :] + ((ex - up_z(ex)) + (ez_n - ez))
            gz = GZ[i, :, :, rows, :] + ((ey - ey_n) + (EX[i - 1, :, :, ahead_rows, :] - ex))
            GX[i, :, :, rows, :] = gx
            GY[i, :, :, rows, :] = gy
            GZ[i, :, :, rows, :] = gz
            if i >= n:
                if i == FIRST:
                    gy_l, gz_l = gy_l * inside, gz_l * inside
                k = K[i - 1, :, rows, :][:, None]
                mask = K[i - 1, 0:1, pl.ds(0, 8), :]
                ex = ex + k * ((gz - GZ[i, :, :, behind_rows, :]) - (gy - down_z(gy)))
                ey = ey + k * add_driven((gx - down_z(gx)) - (gz - gz_l), mask * ih)
                ez = ez + k * add_driven((gy - gy_l) - (gx - GX[i, :, :, behind_rows, :]), mask * ie)
                EX[i - 1, :, :, rows, :] = ex
                EY[i - 1, :, :, rows, :] = ey
                EZ[i - 1, :, :, rows, :] = ez
                if FIRST <= i < FIRST + 2 * DEPTH:
                    GR[i - FIRST, :, rows, :] = GR[i - FIRST, :, rows, :] + (product(ex) + product(ey) + product(ez))
            gy_l, gz_l = gy, gz

    def near_copy(j):
        first, stop = out_chunks[j]
        return remote(
            GR.at[:, 1 - core, ds8(PAD + 8 * (p + first), 8 * (stop - first)), :],
            near.at[:, pl.ds(8 * first, 8 * (stop - first)), :],
            near_send.at[j], near_recv.at[j], s, other_core,
        )

    def far_copies(j):
        first, stop = out_chunks[j]
        rows = pl.ds(8 * first, 8 * (stop - first))
        mine, theirs = pl.ds(DEPTH * p, DEPTH), pl.ds(DEPTH * (1 - p), DEPTH)
        return [
            remote(part.at[mine, rows, :], far.at[:, rows, :], far_send.at[0, j], far_recv.at[0, j], s, other_run),
            remote(part.at[theirs, rows, :], side.at[0, :, rows, :], far_send.at[1, j], far_recv.at[1, j], mate, r),
            remote(
                part.at[theirs, rows, :], side.at[1, :, rows, :], far_send.at[2, j], far_recv.at[2, j], mate, other_run
            ),
        ]

    def fin_copies(j):
        first, stop = out_chunks[j]
        copies = []
        for k in range(2):
            rows = ds8(half * k + 8 * first, 8 * (stop - first))
            src = fin.at[:, rows, :]
            dst = grad_h.at[:, core, rows, :]
            copies.append(
                (
                    pltpu.make_async_copy(src, dst, fin_copy.at[k, j]),
                    remote(src, dst, fin_send.at[k, j], fin_recv.at[k, j], s, other_core),
                    remote(
                        src, grad_h.at[:, 1 - core, rows, :],
                        fin_send.at[k, j], fin_recv.at[k, j], s, other_core,
                    ),
                )
            )
        return copies

    def field_copies(j):
        first, stop = out_chunks[j]
        size = 8 * (stop - first)
        src_rows = ds8(PAD + 8 * (p + first), size)
        dst = out_h.at[:, :, ds8(half * p + 8 * first, size), :]
        back = out_h.at[:, :, ds8(half * (1 - p) + 8 * first, size), :]
        src = EY.at[pl.ds(mates - 1, DEPTH), :, 0, src_rows, :]
        return [
            (
                pltpu.make_async_copy(EY.at[pl.ds(own - 1, DEPTH), :, 0, src_rows, :], dst, fo_copy.at[j]),
                remote(src, dst, fo_send.at[j], fo_recv.at[j], mate, r),
                remote(src, back, fo_send.at[j], fo_recv.at[j], mate, r),
            )
        ]

    def fields_start(j):
        for here, there, _ in field_copies(j):
            there.start()
            here.start()

    def rows_done(j):
        near_copy(j).start()
        if j < len(out_chunks) - 2:
            fields_start(j)

    def sum_cores(j):
        first, stop = out_chunks[j]
        near_copy(j).wait_recv()

        def one(t, carry):
            rows = ds8(8 * t, 8)
            part[:, rows, :] = GR[:, core, ds8(PAD + 8 * (p + t), 8), :] + near[:, rows, :]
            return carry

        lax.fori_loop(first, stop, one, 0)
        for copy in far_copies(j):
            copy.start()
        if j >= len(out_chunks) - 2:
            fields_start(j)

    def sum_chips(j):
        first, stop = out_chunks[j]
        for copy in far_copies(j):
            copy.wait_recv()

        def one(t, carry):
            rows = ds8(8 * t, 8)
            fin[:, ds8(half * p + 8 * t, 8), :] = part[pl.ds(DEPTH * p, DEPTH), rows, :] + far[:, rows, :]
            fin[:, ds8(half * (1 - p) + 8 * t, 8), :] = side[0, :, rows, :] + side[1, :, rows, :]
            return carry

        lax.fori_loop(first, stop, one, 0)
        for here, there, _ in fin_copies(j):
            there.start()
            here.start()

    sweeps = tiles + STEPS - 1
    before, after, late = {}, {}, []
    for c in range(1, len(in_chunks)):
        at = in_chunks[c][0] - 1
        if PASS_AT[c] >= 0:
            before.setdefault(PASS_AT[c], []).append(functools.partial(pass_on, c))
        before.setdefault(max(0, at - 2), []).append(functools.partial(pass_across, c))
        before.setdefault(at, []).append(functools.partial(halo_wait, c))
    for j in range(len(out_chunks)):
        at = out_chunks[j][1] + STEPS - 1
        for event, delay in ((rows_done, 0), (sum_cores, 1), (sum_chips, 5)):
            if at + delay < sweeps:
                after.setdefault(at + delay, []).append(functools.partial(event, j))
            else:
                late.append((at + delay, functools.partial(event, j)))
    late.sort(key=lambda item: item[0])

    def at_sweep(T, table_of):
        for at, events in sorted(table_of.items()):

            @pl.when(T == at)
            def _():
                for event in events:
                    event()

    pass_across(0)
    port_wait()
    halo_wait(0)

    def sweep(T, carry):
        at_sweep(T, before)
        for n in range(1, STEPS + 1):
            t = T - (n - 1)
            high = tiles - 2 + p if n == STEPS else tiles - 1

            @pl.when((t >= 0) & (t <= high))
            def _():
                first_step(t) if n == 1 else later_step(n, t)

        at_sweep(T, after)
        return carry

    lax.fori_loop(0, sweeps, sweep, 0)
    for _, event in late:
        event()

    for j in range(len(out_chunks)):
        for here, there, back in fin_copies(j) + field_copies(j):
            here.wait()
            there.wait_send()
            back.wait_recv()
        near_copy(j).wait_send()
        for copy in far_copies(j):
            copy.wait_send()
    for d in range(1, grid_y):
        y_rows(d, py).wait_send()
    mate_rows(column).wait_send()
    for d in range(1, grid_z):
        z_rows(d, pz).wait_send()

    @pl.when(at_edge(pz))
    def _():
        for d in range(1, grid_z):
            edge_rows(d).wait_send()

    for c in range(len(in_chunks)):
        share(c, 0, core).wait_send()
        for copy in x_copies(c):
            copy.wait_send()

        @pl.when(not_last)
        def _():
            share(c, 2, core).wait_send()
            for kind in range(2):
                for part in range(2):
                    z_copy(c, kind, True, part).wait_send()

        @pl.when(not_first)
        def _():
            share(c, 1, core).wait_send()
            for kind in range(2):
                for part in range(2):
                    z_copy(c, kind, False, part).wait_send()


def local(slabs, grid_y, grid_z, material, eps_table, surface_mask, excite_map, mode_profiles, port_eps, cotangent):
    tiles = slabs // 2 + 1
    height = 8 * tiles + 2 * PAD
    half, rows = 4 * slabs, 8 * slabs
    chunks, outs = len(cuts(tiles, IN_SIZES)), len(cuts(tiles - 1, OUT_SIZES))
    vmem = lambda *shape: pltpu.VMEM(shape, F32)
    dma = lambda *shape: pltpu.SemaphoreType.DMA(shape)
    field = lambda layers: vmem(layers, 2, 2, height, 128)
    smem_spec = pl.BlockSpec(memory_space=pltpu.SMEM)
    vmem_spec = pl.BlockSpec(memory_space=pltpu.VMEM)
    any_spec = pl.BlockSpec(memory_space=pl.ANY)
    scratch = [
        vmem(LAYERS, 2, height, 128),
        vmem(LAYERS - 2, 2, height, 128),
        vmem(DEPTH, 2, height, 128),
        vmem(DEPTH, height, 128),
        pltpu.VMEM((DEPTH, rows, 256), jnp.int32),
        vmem(DEPTH, rows, 256),
        field(LAYERS - 2), field(LAYERS - 2), field(LAYERS - 2),
        field(LAYERS - 1), field(LAYERS - 1), field(LAYERS - 1),
        vmem(2 * DEPTH, 2, height, 128),
        vmem(STEPS, 2, height, 128),
        vmem(grid_y, 2 * grid_z, 4, 8, 128),
        vmem(2 * DEPTH, half, 128), vmem(2 * DEPTH, half, 128),
        vmem(DEPTH, half, 128), vmem(2, DEPTH, half, 128), vmem(DEPTH, rows, 128),
        dma(2), dma(grid_y + 2 * grid_z - 2), dma(grid_y + 2 * grid_z - 2),
        dma(chunks), dma(chunks), dma(chunks), dma(chunks), dma(2, 4, chunks), dma(2, 4, chunks),
        dma(3, chunks), dma(3, chunks),
        dma(outs), dma(outs), dma(3, outs), dma(3, outs),
        dma(2, outs), dma(2, outs), dma(2, outs), dma(outs), dma(outs), dma(outs),
    ]
    split = jax.ShapeDtypeStruct((DEPTH, 2, rows, 128), F32)
    grad_p, field_p = pl.pallas_call(
        functools.partial(kernel, slabs, grid_y, grid_z),
        out_shape=(split, split),
        in_specs=[smem_spec, smem_spec, smem_spec, vmem_spec, vmem_spec, any_spec, any_spec],
        out_specs=(any_spec, any_spec),
        scratch_shapes=scratch,
        compiler_params=pltpu.CompilerParams(
            collective_id=0, has_side_effects=True, vmem_limit_bytes=60 * 1024 * 1024
        ),
        cost_estimate=pl.CostEstimate(flops=600_000_000, bytes_accessed=6_000_000, transcendentals=0),
    )(eps_table, surface_mask, excite_map, mode_profiles, port_eps, material, cotangent)
    halves = pl.BlockSpec((1, 2, half, 128), lambda x, y: (x, 0, y, 0))
    return pl.pallas_call(
        restore,
        grid=(DEPTH, 2),
        out_shape=(
            jax.ShapeDtypeStruct(material.shape, F32),
            jax.ShapeDtypeStruct(cotangent.shape, F32),
        ),
        in_specs=[halves, halves],
        out_specs=(
            pl.BlockSpec((1, half, 256), lambda x, y: (x, y, 0)),
            pl.BlockSpec((1, 1, half, 256), lambda x, y: (0, x, y, 0)),
        ),
        compiler_params=pltpu.CompilerParams(vmem_limit_bytes=60 * 1024 * 1024),
    )(grad_p, field_p)


def solution(mesh):
    slabs = mesh.shape["slab"]
    grid_z = 4 if slabs == 32 else 2
    grid_y = slabs // 2 // grid_z
    in_specs = (
        P("slab", None, None),
        P(),
        P("slab"),
        P("run"),
        P(None, "slab", None),
        P("slab", None),
        P("run", "slab", None, None),
    )
    out_specs = (P("slab", None, None), P("run", "slab", None, None))
    return jax.shard_map(
        functools.partial(local, slabs, grid_y, grid_z),
        mesh=mesh, in_specs=in_specs, out_specs=out_specs, check_vma=False,
    )
```
